32 devices in a mesh: dp: 2 (over x), seq: 4 (over y, core), expert: 4 (over z).
Axes of the slice: x: 2, y: 2, z: 4, core: 2. Of those that a mesh axis runs over, the one named last changes fastest.
Arguments:
- tokens: bfloat16 [8, 1024, 768], P(('dp', 'expert'), 'seq'), may hold values from -6 to 6
- qkv_weight: bfloat16 [768, 2304], P(('dp', 'seq', 'expert')), may hold values from -0.21875 to 0.21875
- out_weight: bfloat16 [768, 768], P(('dp', 'seq', 'expert')), may hold values from -1.75 to 1.75
- router_weight: bfloat16 [768, 4], P(('dp', 'seq', 'expert')), may hold values from -0.15625 to 0.15625
- w_in: bfloat16 [4, 768, 3072], P('expert', ('dp', 'seq')), may hold values from -0.21875 to 0.21875
- w_out: bfloat16 [4, 3072, 768], P('expert', None, ('dp', 'seq')), may hold values from -0.109375 to 0.109375
- norm_gains: float32 [2, 768], replicated, may hold values from 0.5 to 1.5
- bias_table: float32 [32, 12], replicated, may hold values from -4 to 4
- expert_ids: int32 [8, 1024, 2], P(('dp', 'expert'), 'seq'), may hold values from 0 to 3, all different within a row; in each aligned block of 256 rows (0 to 255, 256 to 511, ..., all dimensions but the last counted through in order) at most 192 rows name the same one
- cotangent: bfloat16 [8, 1024, 768], P(('dp', 'expert'), 'seq'), may hold values from -6 to 6
Outputs:
- layer_out: bfloat16 [8, 1024, 768], P(('dp', 'expert'), 'seq')
- input_grad: bfloat16 [8, 1024, 768], P(('dp', 'expert'), 'seq')
- qkv_grad: float32 [768, 2304], P(('dp', 'seq', 'expert'))
- out_grad: float32 [768, 768], P(('dp', 'seq', 'expert'))
- router_grad: float32 [768, 4], P(('dp', 'seq', 'expert'))
- w_in_grad: float32 [4, 768, 3072], P('expert', ('dp', 'seq'))
- w_out_grad: float32 [4, 3072, 768], P('expert', None, ('dp', 'seq'))
- gains_grad: float32 [2, 768], replicated
- table_grad: float32 [32, 12], replicated
The draws below stay inside these ranges and needn't reach their ends.
Inputs may be any that keep to these rules, and one draw needn't show every extreme that they name: `expert_ids`: the two experts of a token differ. Within the 256 rows of one device (aligned blocks of 256 positions of a sequence) no expert is named more than 192 times, a bound that some block reaches.
All inputs are finite; a program needn't handle non-finite values.
Results may differ from the reference program's by a relative error of at most 0.015.
Values may be sent and summed in bfloat16 or wider, within the bound.
A program may use at most 128 MiB of HBM per device.

```python
import math
import jax
import jax.numpy as jnp
import numpy as np
from jax import lax

D = 768
HEADS = 12
HEAD_DIM = 64
FF = 3072
BUCKETS = 32
LEN_DEV = 256
LEN = 1024
SEQS = 8
EXPERTS = 4
CAP = 192
N_SEQ = 4


def strengthened(values, key, source, target, shards_of, factor):
    def block_of(position):
        return (jnp.arange(values.shape[position]) // (values.shape[position] // shards_of)).reshape((-1,) + (1,) * (values.ndim - 1 - position))

    one_side = jax.random.permutation(key, shards_of)[block_of(target)]
    other_side = (block_of(target) + shards_of // 2) % shards_of
    return jnp.where((block_of(source) == one_side) | (block_of(source) == other_side), factor * values, values)


def shard_levels(rng, shape, shards, low, largest):
    factor_of, own = 1.0, jax.random.fold_in(rng, 6)
    for dim, parts in shards:
        draws = jnp.exp(jax.random.uniform(jax.random.fold_in(own, dim), (parts,), jnp.float32, low / len(shards), largest / len(shards)))
        factor_of = factor_of * jnp.repeat(draws, shape[dim] // parts).reshape([-1 if axis == dim else 1 for axis in range(len(shape))])
    return factor_of


def shared_out(key, own, number, rows, count, top, limit, skew):
    sequence = jax.random.permutation(key, count)
    crowded, common = load_shares(count, rows * top, limit, skew, True), load_shares(count, rows * top, limit, skew, False)
    places = jnp.arange(count)

    def named(tallies, rotation):
        used = int((tallies > 0).sum())
        fixed = max(1, used // 4)
        passed = fixed + (places - fixed + rotation * (used - fixed)) % max(1, count - fixed)
        return jnp.zeros((count,), jnp.int32).at[sequence[jnp.where(places < fixed, places, passed)]].set(jnp.asarray(tallies, jnp.int32))

    tallies = jnp.where(number % 4 == 0, named(crowded, number // 4), named(common, number - number // 4 - 1))
    mixed = jax.random.permutation(jax.random.fold_in(own, 3), count)
    source_of, receiver = mixed[0:count // 2 * 2:2], mixed[1:count // 2 * 2:2]
    slack = jnp.minimum(tallies[source_of] - 1, limit - tallies[receiver]) // 2
    slack = jnp.where((source_of == sequence[0]) | (receiver == sequence[0]) | (tallies[receiver] == 0), 0, jnp.maximum(slack, 0))
    passed = jax.random.randint(jax.random.fold_in(own, 4), (count // 2,), 0, 1 << 20) % (slack + 1)
    tallies = tallies.at[source_of].add(-passed).at[receiver].add(passed)
    labels = jnp.searchsorted(jnp.cumsum(tallies), jnp.arange(rows * top), side="right").astype(jnp.int32)
    grid = labels.reshape(top, rows).T
    grid = grid[jax.random.permutation(jax.random.fold_in(own, 1), rows)]
    rotation = jax.random.randint(jax.random.fold_in(own, 2), (rows, 1), 0, top)
    return jnp.take_along_axis(grid, (jnp.arange(top)[None, :] + rotation) % top, axis=1)


def load_shares(count, total, bound, skew, full):
    weights = [(1 << 20) // math.isqrt(standing ** skew) + 1 for standing in range(1, count + 1)]
    largest = bound if full else min(bound, max(-(-total // count), total * weights[0] // sum(weights)))
    least = 1 if total - largest >= count - 1 else 0
    holding, surplus = [largest] + [least] * (count - 1), total - largest - least * (count - 1)
    while surplus > 0:
        candidates = [i for i in range(1, count) if holding[i] < largest] or [i for i in range(1, count) if holding[i] < bound]
        mass, left = sum([weights[i] for i in candidates]), surplus
        for i in candidates:
            more = min(bound - holding[i], max(1, left * weights[i] // mass), surplus)
            holding[i] = holding[i] + more
            surplus = surplus - more
    return np.array(holding)


def noise(rng, extent, scale, reach, shards=(), held_as=jnp.bfloat16):
    factor_of = shard_levels(rng, extent, shards, -0.22, 0.18) if shards else 1.0
    array = jax.random.normal(rng, extent, jnp.float32) * scale * factor_of
    return jnp.minimum(jnp.maximum(array, -reach), reach).astype(held_as)


def noise_with(rng, extent, spread, most, pieces, heavy, held_as=jnp.bfloat16):
    entries = spread * jax.random.normal(rng, extent, jnp.float32)
    if pieces:
        entries = entries * shard_levels(rng, extent, pieces, -0.22, 0.18)
    return jnp.clip(strengthened(entries, jax.random.fold_in(rng, 3), *heavy), -most, most).astype(held_as)


def setup_inputs(seed: int = 0) -> dict:
    streams_of = jax.random.split(jax.random.key(seed), 11)
    tokens = noise_with(streams_of[0], (SEQS, LEN, D), 1.0, 6.0, ((0, 8), (1, 4)), (0, 2, 8, 2.0))
    qkv_weight = noise(streams_of[1], (D, 3 * D), D ** -0.5, 0.21875, ((0, 32),))
    out_weight = noise(streams_of[2], (D, D), (D // 64) ** -0.5, 1.75, ((0, 32),))
    router_weight = noise(streams_of[3], (D, EXPERTS), (2 * D) ** -0.5, 0.15625, ((0, 32),))
    w_in = noise(streams_of[4], (EXPERTS, D, FF), D ** -0.5, 0.21875, ((0, 4), (1, 8)))
    w_out = noise(streams_of[5], (EXPERTS, FF, D), FF ** -0.5, 0.109375, ((0, 4), (2, 8)))
    norm_gains = jnp.clip(1.0 + 0.1 * jax.random.normal(streams_of[6], (2, D), jnp.float32), 0.5, 1.5)
    bias_table = noise(streams_of[7], (BUCKETS, HEADS), 1.0, 4.0, (), jnp.float32)
    expert_ids_keys = jax.random.split(jax.random.fold_in(streams_of[8], 1), SEQS * LEN // LEN_DEV)
    expert_ids_turns = jax.random.permutation(jax.random.fold_in(streams_of[8], 3), SEQS * LEN // LEN_DEV)
    expert_ids = jax.vmap(lambda own, number: shared_out(jax.random.fold_in(streams_of[8], 2), own, number, LEN_DEV, EXPERTS, 2, CAP, 1))(expert_ids_keys, expert_ids_turns).reshape((SEQS, LEN, 2))
    cotangent = noise(streams_of[9], (SEQS, LEN, D), 1.0, 6.0, ((0, 8), (1, 4)))
    return {"tokens": tokens, "qkv_weight": qkv_weight, "out_weight": out_weight, "router_weight": router_weight, "w_in": w_in, "w_out": w_out, "norm_gains": norm_gains, "bias_table": bias_table, "expert_ids": expert_ids, "cotangent": cotangent}


EPS = 1e-06
HIGH_PRECISION = lax.Precision.HIGHEST

@jax.custom_vjp
def low(v):
    return lax.optimization_barrier(v.astype(jnp.bfloat16)).astype(jnp.float32)

@jax.custom_vjp
def low_back(v):
    return v

def low_keep(v):
    return (low(v), None)

def low_pass(kept, grad):
    return (grad,)

def back_keep(v):
    return (v, None)

def back_low(kept, grad):
    return (low(grad),)
low.defvjp(low_keep, low_pass)
low_back.defvjp(back_keep, back_low)

def rounded_pair(values):
    return low_back(low(values))

def bucket_edges(bucket_count):
    exact_count = bucket_count // 2
    boundaries = list(range(1, exact_count + 1))
    for bucket_index in range(exact_count + 1, bucket_count):
        power = (bucket_index - exact_count) / (bucket_count - exact_count)
        boundaries.append(math.ceil(exact_count * (128.0 / exact_count) ** power))
    return boundaries

def bucket_ids(distance, bucket_count):
    distance = jnp.maximum(distance, 0)
    bucket_sum = jnp.zeros(distance.shape, jnp.int32)
    for boundary in bucket_edges(bucket_count):
        bucket_sum = bucket_sum + (distance >= boundary).astype(jnp.int32)
    return bucket_sum

def rms_norm(values, scale_gain):
    return values * lax.rsqrt(lax.optimization_barrier(jnp.mean(values * values, axis=-1, keepdims=True)) + EPS) * scale_gain

def attend_head(operands, buckets, causal):
    queries, key_part, value_part, column = operands
    scores = jnp.dot(queries, key_part.T, precision=HIGH_PRECISION) * HEAD_DIM ** (-0.5) + column[buckets]
    scores = jnp.where(causal, low_back(scores), -1e+30)
    probabilities = jax.nn.softmax(scores, axis=-1)
    return jnp.dot(low(probabilities), value_part, precision=HIGH_PRECISION)

def attend_sequence(one_sequence, bias_table, buckets, causal):
    head_parts = one_sequence.reshape(LEN, 3, HEADS, HEAD_DIM).transpose(1, 2, 0, 3)

    def one_head(operands):
        return attend_head(operands, buckets, causal)
    head_outputs = lax.map(jax.checkpoint(one_head), (head_parts[0], head_parts[1], head_parts[2], bias_table.T))
    return head_outputs.transpose(1, 0, 2).reshape(LEN, HEADS * HEAD_DIM)

def run_expert(operands):
    rows_in, first_weight, second_weight = operands
    hidden_pre = low_back(jnp.dot(rows_in, first_weight, precision=HIGH_PRECISION))
    hidden_rows = low(jax.nn.gelu(hidden_pre))
    return jnp.dot(hidden_rows, second_weight, precision=HIGH_PRECISION)

def forward(inputs, query_key_value_matrix, output_matrix, router_matrix, first_w, second_w, norm_gains, bias_table, expert_ids, buckets, causal):
    normalized_rows = low(rms_norm(inputs, norm_gains[0]))
    projected_rows = rounded_pair(jnp.einsum('mif,fc->mic', normalized_rows, query_key_value_matrix, precision=HIGH_PRECISION))

    def one_sequence(sequence_rows):
        return attend_sequence(sequence_rows, bias_table, buckets, causal)
    attention_result = rounded_pair(lax.map(jax.checkpoint(one_sequence), projected_rows))
    residual_branch = low_back(jnp.einsum('mif,fc->mic', attention_result, output_matrix, precision=HIGH_PRECISION))
    middle = inputs + residual_branch
    combined_rows = low(rms_norm(middle, norm_gains[1]))
    router_logits = jnp.einsum('mif,fc->mic', combined_rows, router_matrix, precision=HIGH_PRECISION)
    choose = (expert_ids[..., None] == jnp.arange(EXPERTS, dtype=jnp.int32)).astype(jnp.float32)
    chosen = lax.optimization_barrier(jnp.sum(choose * router_logits[:, :, None, :], axis=-1))
    gate_weights = jax.nn.softmax(chosen, axis=-1)
    block_total = SEQS * N_SEQ
    copies = low_back(jnp.broadcast_to(combined_rows[:, :, None, :], (SEQS, LEN, 2, D)))
    copies = copies.reshape(block_total, LEN_DEV * 2, D)
    flat_ids = expert_ids.reshape(block_total, LEN_DEV * 2)
    expert_hits = (flat_ids[..., None] == jnp.arange(EXPERTS, dtype=jnp.int32)).astype(jnp.int32)
    slot_rank = lax.optimization_barrier(jnp.sum((jnp.cumsum(expert_hits, axis=1) - 1) * expert_hits, axis=-1))
    places = (flat_ids * CAP + slot_rank).astype(jnp.int32)
    block_index = jnp.arange(block_total, dtype=jnp.int32)[:, None]
    buffer = jnp.zeros((block_total, EXPERTS * CAP, D), jnp.float32).at[block_index, places].set(copies)
    per_expert = buffer.reshape(block_total, EXPERTS, CAP, D).transpose(1, 0, 2, 3).reshape(EXPERTS, block_total * CAP, D)
    results = rounded_pair(lax.map(jax.checkpoint(run_expert), (per_expert, first_w, second_w)))
    returned_buffer = results.reshape(EXPERTS, block_total, CAP, D).transpose(1, 0, 2, 3).reshape(block_total, EXPERTS * CAP, D)
    returned = returned_buffer[block_index, places].reshape(SEQS, LEN, 2, D)
    expert_sum = lax.optimization_barrier(jnp.sum(gate_weights[..., None] * returned, axis=2))
    return middle + expert_sum

def reference(tokens, qkv_weight, out_weight, router_weight, w_in, w_out, norm_gains, bias_table, expert_ids, cotangent):
    positions = jnp.arange(LEN, dtype=jnp.int32)
    distance = positions[:, None] - positions[None, :]
    causal = distance >= 0
    buckets = bucket_ids(distance, BUCKETS)

    def closed(inputs, query_key_value_matrix, output_matrix, router_matrix, first_w, second_w, gains, table):
        return forward(inputs, query_key_value_matrix, output_matrix, router_matrix, first_w, second_w, gains, table, expert_ids, buckets, causal)
    output, pullback = jax.vjp(closed, tokens.astype(jnp.float32), qkv_weight.astype(jnp.float32), out_weight.astype(jnp.float32), router_weight.astype(jnp.float32), w_in.astype(jnp.float32), w_out.astype(jnp.float32), norm_gains, bias_table)
    grads = pullback(cotangent.astype(jnp.float32))
    return (output.astype(jnp.bfloat16), grads[0].astype(jnp.bfloat16), grads[1], grads[2], grads[3], grads[4], grads[5], grads[6], grads[7])
```

```python
import functools
import math

import jax
import jax.numpy as jnp
from jax import lax
from jax.experimental import pallas as pl
from jax.experimental.pallas import tpu as pltpu
from jax.sharding import PartitionSpec as P

D = 768
HEADS = 12
HEAD_DIM = 64
FF = 3072
BUCKETS = 32
LEN_DEV = 256


EPS = 1e-06
HIGH_PRECISION = lax.Precision.HIGHEST
CONTRACT_ROWS = (((0,), (0,)), ((), ()))


def bucket_edges(bucket_count):
    exact_count = bucket_count // 2
    boundaries = list(range(1, exact_count + 1))
    for bucket_index in range(exact_count + 1, bucket_count):
        power = (bucket_index - exact_count) / (bucket_count - exact_count)
        boundaries.append(math.ceil(exact_count * (128.0 / exact_count) ** power))
    return boundaries


def bucket_ids(distance, bucket_count):
    distance = jnp.maximum(distance, 0)
    bucket_sum = jnp.zeros(distance.shape, jnp.int32)
    for boundary in bucket_edges(bucket_count):
        bucket_sum = bucket_sum + (distance >= boundary).astype(jnp.int32)
    return bucket_sum


def norm_forward(values, scale_gain):
    inverse = lax.rsqrt(jnp.mean(values * values, axis=-1, keepdims=True) + EPS)
    normal_rows = values * inverse
    return (normal_rows * scale_gain, normal_rows, inverse)


def norm_backward(grad_out, normal_rows, inverse, scale_gain):
    gain_part = jnp.sum(grad_out * normal_rows, axis=0)
    scaled = grad_out * scale_gain
    value_grad = inverse * (
        scaled - normal_rows * jnp.mean(scaled * normal_rows, axis=-1, keepdims=True)
    )
    return (value_grad, gain_part)


def to_slots(slot_table, rows):
    return jnp.dot(slot_table, rows, preferred_element_type=jnp.float32).astype(jnp.bfloat16)


def from_slots(slot_table, rows):
    return lax.dot_general(slot_table, rows, CONTRACT_ROWS, preferred_element_type=jnp.float32)


TILE = 128
PAIR = 128
MASKED = -1e30
MATMUL_NT = (((1,), (1,)), ((), ()))


def matmul(left, right, dims=(((1,), (0,)), ((), ()))):
    return lax.dot_general(left, right, dims, preferred_element_type=jnp.float32)


def band_distance():
    key_row = lax.broadcasted_iota(jnp.int32, (2 * TILE, TILE), 0)
    query_column = lax.broadcasted_iota(jnp.int32, (2 * TILE, TILE), 1)
    return TILE + query_column - key_row


def fill_bias(strip, table_ref, head, tiles):
    distance = band_distance()
    band = jnp.full((2 * TILE, TILE), table_ref[0, head], jnp.float32)
    for bucket, edge in enumerate(bucket_edges(BUCKETS)):
        band = jnp.where(distance >= edge, table_ref[bucket + 1, head], band)
    band = jnp.where(distance >= 0, band, MASKED)
    far = (tiles - 2) * TILE
    strip[0:far, :] = jnp.full((far, TILE), table_ref[BUCKETS - 1, head], jnp.float32)
    strip[far : far + 2 * TILE, :] = band


def head_probabilities(strip, place, queries, keys, tiles):
    scores = matmul(keys, queries, MATMUL_NT)
    columns = []
    for part in range(LEN_DEV // TILE):
        start = (tiles - 1 - part) * TILE - place * LEN_DEV
        columns.append(strip[pl.ds(pl.multiple_of(start, TILE), tiles * TILE), :])
    scores = scores + jnp.concatenate(columns, axis=1)
    exps = jnp.exp(scores - jnp.max(scores, axis=0, keepdims=True))
    return exps * (1.0 / jnp.sum(exps, axis=0, keepdims=True))


def lane_halves(shape):
    return lax.broadcasted_iota(jnp.int32, shape, 1) < HEAD_DIM


def attend_kernel(tiles, place_ref, table_ref, q_ref, k_ref, v_ref, out_ref, strip):
    pair = pl.program_id(0)
    place = place_ref[0]

    @pl.when(pair == 0)
    def _():
        strip[tiles * TILE :, :] = jnp.full(((tiles - 1) * TILE, TILE), MASKED, jnp.float32)

    keys, values = k_ref[...], v_ref[...]
    queries = q_ref[...] * jnp.bfloat16(HEAD_DIM**-0.5)
    first = lane_halves(queries.shape)
    zero = jnp.zeros_like(queries)
    results = []
    for half in range(2):
        fill_bias(strip, table_ref, pair * 2 + half, tiles)
        own = jnp.where(first, queries, zero) if half == 0 else jnp.where(first, zero, queries)
        probs = head_probabilities(strip, place, own, keys, tiles).astype(jnp.bfloat16)
        results.append(matmul(values, probs, CONTRACT_ROWS))
    top = lax.broadcasted_iota(jnp.int32, results[0].shape, 0) < HEAD_DIM
    out_ref[...] = jnp.where(top, results[0], results[1]).T.astype(out_ref.dtype)


def attend_back_kernel(
    tiles, place_ref, table_ref, q_ref, k_ref, v_ref, g_ref, dq_ref, dkv_ref, sums_ref, strip, held
):
    pair = pl.program_id(0)
    place = place_ref[0]

    @pl.when(pair == 0)
    def _():
        strip[tiles * TILE :, :] = jnp.full(((tiles - 1) * TILE, TILE), MASKED, jnp.float32)

    keys, values = k_ref[...], v_ref[...]
    queries = q_ref[...] * jnp.bfloat16(HEAD_DIM**-0.5)
    grads = g_ref[...]
    first = lane_halves(queries.shape)
    zero = jnp.zeros_like(queries)
    distance = band_distance()
    buckets = jnp.full(distance.shape, -1, jnp.int32)
    for bucket, edge in enumerate([0] + bucket_edges(BUCKETS)):
        buckets = jnp.where(distance >= edge, bucket, buckets)
    q_parts, k_parts, v_parts = [], [], []
    for half in range(2):
        fill_bias(strip, table_ref, pair * 2 + half, tiles)
        own = jnp.where(first, queries, zero) if half == 0 else jnp.where(first, zero, queries)
        own_grads = jnp.where(first, grads, zero) if half == 0 else jnp.where(first, zero, grads)
        probs = head_probabilities(strip, place, own, keys, tiles)
        prob_grad = matmul(values, own_grads, MATMUL_NT)
        dots = jnp.sum(probs * prob_grad, axis=0, keepdims=True)
        score_grad = (probs * (prob_grad - dots)).astype(jnp.bfloat16)
        held[...] = score_grad
        k_parts.append(matmul(score_grad, queries))
        v_parts.append(matmul(probs.astype(jnp.bfloat16), grads))
        q_parts.append(matmul(keys, score_grad, CONTRACT_ROWS))
        band = jnp.zeros((2 * TILE, TILE), jnp.float32)
        for part in range(LEN_DEV // TILE):
            tile = place * (LEN_DEV // TILE) + part
            before = jnp.maximum(tile - 1, 0)
            cols = slice(part * TILE, (part + 1) * TILE)
            near = held[pl.ds(pl.multiple_of(before * TILE, TILE), TILE), cols].astype(jnp.float32)
            same = held[pl.ds(pl.multiple_of(tile * TILE, TILE), TILE), cols].astype(jnp.float32)
            near = jnp.where(tile > 0, near, 0.0)
            band = band + jnp.concatenate([near, same], axis=0)
        total = jnp.sum(score_grad.astype(jnp.float32), axis=0, keepdims=True)
        total = total[:, :TILE] + total[:, TILE:]
        far = total - jnp.sum(band, axis=0, keepdims=True)
        for bucket in range(BUCKETS):
            row = jnp.sum(jnp.where(buckets == bucket, band, 0.0), axis=0, keepdims=True)
            if bucket == BUCKETS - 1:
                row = row + far
            sums_ref[half, bucket : bucket + 1, :] = row
    top = lax.broadcasted_iota(jnp.int32, q_parts[0].shape, 0) < HEAD_DIM
    dq = jnp.where(top, q_parts[0], q_parts[1]).T * HEAD_DIM**-0.5
    dq_ref[...] = dq.astype(dq_ref.dtype)
    side = lane_halves(k_parts[0].shape)
    dkv_ref[0] = jnp.where(side, k_parts[0], k_parts[1]).astype(dkv_ref.dtype)
    dkv_ref[1] = jnp.where(side, v_parts[0], v_parts[1]).astype(dkv_ref.dtype)


def attention_specs(full_length):
    pairs = D // PAIR
    smem = pl.BlockSpec(memory_space=pltpu.SMEM)
    rows = pl.BlockSpec((LEN_DEV, PAIR), lambda pair: (0, pair))
    keys = pl.BlockSpec((full_length, PAIR), lambda pair: (0, pair))
    values = pl.BlockSpec((full_length, PAIR), lambda pair: (0, pair + pairs))
    return pairs, smem, rows, keys, values


def attend(place, bias_table, projected, key_values):
    full_length = key_values.shape[0]
    tiles = full_length // TILE
    pairs, smem, rows, keys, values = attention_specs(full_length)
    return pl.pallas_call(
        functools.partial(attend_kernel, tiles),
        grid=(pairs,),
        out_shape=jax.ShapeDtypeStruct((LEN_DEV, D), jnp.bfloat16),
        in_specs=[smem, smem, rows, keys, values],
        out_specs=rows,
        scratch_shapes=[pltpu.VMEM(((2 * tiles - 1) * TILE, TILE), jnp.float32)],
        compiler_params=pltpu.CompilerParams(vmem_limit_bytes=40 * 2**20),
        cost_estimate=pl.CostEstimate(
            flops=4 * LEN_DEV * full_length * PAIR * HEADS,
            bytes_accessed=2 * D * (2 * LEN_DEV + 2 * full_length),
            transcendentals=HEADS * LEN_DEV * full_length,
        ),
    )(place, bias_table, projected, key_values, key_values)


def attend_back(place, bias_table, projected, key_values, attended_grad):
    full_length = key_values.shape[0]
    tiles = full_length // TILE
    pairs, smem, rows, keys, values = attention_specs(full_length)
    return pl.pallas_call(
        functools.partial(attend_back_kernel, tiles),
        grid=(pairs,),
        out_shape=(
            jax.ShapeDtypeStruct((LEN_DEV, D), jnp.bfloat16),
            jax.ShapeDtypeStruct((2, full_length, D), jnp.bfloat16),
            jax.ShapeDtypeStruct((HEADS, BUCKETS, TILE), jnp.float32),
        ),
        in_specs=[smem, smem, rows, keys, values, rows],
        out_specs=(
            rows,
            pl.BlockSpec((2, full_length, PAIR), lambda pair: (0, 0, pair)),
            pl.BlockSpec((2, BUCKETS, TILE), lambda pair: (pair, 0, 0)),
        ),
        scratch_shapes=[
            pltpu.VMEM(((2 * tiles - 1) * TILE, TILE), jnp.float32),
            pltpu.VMEM((full_length, LEN_DEV), jnp.bfloat16),
        ],
        compiler_params=pltpu.CompilerParams(vmem_limit_bytes=48 * 2**20),
        cost_estimate=pl.CostEstimate(
            flops=10 * LEN_DEV * full_length * PAIR * HEADS,
            bytes_accessed=2 * D * (3 * LEN_DEV + 4 * full_length),
            transcendentals=HEADS * LEN_DEV * full_length,
        ),
    )(place, bias_table, projected, key_values, key_values, attended_grad)


def swap_experts(slots, experts_total):
    return lax.all_to_all(
        slots.reshape(experts_total, slots.shape[0] // experts_total, slots.shape[1]),
        "expert",
        split_axis=0,
        concat_axis=0,
        tiled=True,
    ).reshape(slots.shape)


def local(
    tokens,
    qkv_weight,
    out_weight,
    router_weight,
    w_in,
    w_out,
    norm_gains,
    bias_table,
    expert_ids,
    cotangent,
):
    everywhere = ("dp", "seq", "expert")
    inputs = tokens[0].astype(jnp.float32)
    experts_total = lax.axis_size("expert")
    capacity = 3 * LEN_DEV // experts_total
    router_pad = jnp.zeros((router_weight.shape[0], PAIR - experts_total), jnp.bfloat16)
    packed = jnp.concatenate([qkv_weight, out_weight, router_weight, router_pad], axis=1)
    packed = lax.all_gather(packed, everywhere, axis=0, tiled=True)
    qkv_full, out_full = packed[:, : 3 * D], packed[:, 3 * D : 4 * D]
    router_full = packed[:, 4 * D : 4 * D + experts_total]

    route_ids = expert_ids[0]
    expert_names = jnp.arange(experts_total, dtype=jnp.int32)
    choose = (route_ids[..., None] == expert_names).astype(jnp.float32)
    flat_ids = route_ids.reshape(-1)
    expert_hits = (flat_ids[:, None] == expert_names).astype(jnp.int32)
    slot_rank = jnp.sum((jnp.cumsum(expert_hits, axis=0) - 1) * expert_hits, axis=-1)
    places = (flat_ids * capacity + slot_rank).reshape(LEN_DEV, 2)
    slot_index = jnp.arange(experts_total * capacity, dtype=jnp.int32)[:, None]
    hits = [slot_index == places[None, :, k] for k in range(2)]
    tables = [hit.astype(jnp.bfloat16) for hit in hits]
    token_table = (hits[0] | hits[1]).astype(jnp.bfloat16)
    arrived_cotangent = swap_experts(to_slots(token_table, cotangent[0]), experts_total)

    normalized_rows, normal_one, inverse_one = norm_forward(inputs, norm_gains[0])
    normed_low = normalized_rows.astype(jnp.bfloat16)
    projected_rows = jnp.dot(normed_low, qkv_full, preferred_element_type=jnp.float32).astype(
        jnp.bfloat16
    )
    key_values = lax.all_gather(projected_rows[:, D:], "seq", axis=0, tiled=True)
    place = lax.axis_index("seq").astype(jnp.int32).reshape(1)
    attended_low = attend(place, bias_table, projected_rows, key_values)
    w_in_full = lax.all_gather(w_in, ("dp", "seq"), axis=1, tiled=True)[0]
    w_out_full = lax.all_gather(w_out, ("dp", "seq"), axis=2, tiled=True)[0]
    middle = inputs + jnp.dot(attended_low, out_full, preferred_element_type=jnp.float32)
    mixed, normal_two, inverse_two = norm_forward(middle, norm_gains[1])
    mixed_low = mixed.astype(jnp.bfloat16)
    expert_rows = swap_experts(to_slots(token_table, mixed_low), experts_total)
    router_logits = jnp.dot(mixed_low, router_full, preferred_element_type=jnp.float32)
    chosen = jnp.sum(choose * router_logits[:, None, :], axis=-1)
    gate_weights = jax.nn.softmax(chosen, axis=-1)
    gate_slots = jnp.sum(
        jnp.where(hits[0], gate_weights[None, :, 0], 0.0)
        + jnp.where(hits[1], gate_weights[None, :, 1], 0.0),
        axis=1,
    )
    arrived_gates = lax.all_to_all(
        gate_slots.reshape(experts_total, capacity),
        "expert",
        split_axis=0,
        concat_axis=0,
        tiled=True,
    ).reshape(-1, 1)
    pre_act = jnp.dot(expert_rows, w_in_full, preferred_element_type=jnp.float32)
    hidden_low = jax.nn.gelu(pre_act).astype(jnp.bfloat16)
    expert_out = jnp.dot(hidden_low, w_out_full, preferred_element_type=jnp.float32).astype(
        jnp.bfloat16
    )
    returned = swap_experts(expert_out, experts_total)
    arrived_grad = (arrived_gates * arrived_cotangent.astype(jnp.float32)).astype(jnp.bfloat16)
    hidden_grad = jnp.einsum(
        "rd,fd->rf", arrived_grad, w_out_full, preferred_element_type=jnp.float32
    )
    gelu_value, gelu_pull = jax.vjp(jax.nn.gelu, pre_act)
    pre_grad = gelu_pull(hidden_grad)[0].astype(jnp.bfloat16)
    row_grad = jnp.einsum(
        "rf,df->rd", pre_grad, w_in_full, preferred_element_type=jnp.float32
    ).astype(jnp.bfloat16)
    returned_grad = swap_experts(row_grad, experts_total)
    first_term = lax.dot_general(
        expert_rows, pre_grad, CONTRACT_ROWS, preferred_element_type=jnp.float32
    ).astype(jnp.bfloat16)
    second_term = lax.dot_general(
        arrived_grad, hidden_low, CONTRACT_ROWS, preferred_element_type=jnp.float32
    ).astype(jnp.bfloat16)

    upstream = cotangent[0].astype(jnp.float32)
    gathered = [from_slots(table, returned) for table in tables]
    block_out = middle + gate_weights[:, :1] * gathered[0] + gate_weights[:, 1:] * gathered[1]
    layer_out = block_out.astype(jnp.bfloat16)[None]
    gate_grad = jnp.stack([jnp.sum(upstream * rows, axis=-1) for rows in gathered], axis=-1)
    gate_mean = jnp.sum(gate_weights * gate_grad, axis=-1, keepdims=True)
    chosen_grad = gate_weights * (gate_grad - gate_mean)
    logit_grad = jnp.sum(choose * chosen_grad[..., None], axis=1)
    router_part = lax.dot_general(
        mixed_low.astype(jnp.float32), logit_grad, CONTRACT_ROWS, precision=HIGH_PRECISION
    )
    copy_back = from_slots(token_table, returned_grad)
    mixed_grad = copy_back + jnp.dot(
        logit_grad, router_full.astype(jnp.float32).T, precision=HIGH_PRECISION
    )
    middle_norm_grad, gain_two = norm_backward(mixed_grad, normal_two, inverse_two, norm_gains[1])
    middle_grad = upstream + middle_norm_grad
    branch_low = middle_grad.astype(jnp.bfloat16)
    attended_grad = jnp.einsum(
        "qe,de->qd", branch_low, out_full, preferred_element_type=jnp.float32
    ).astype(jnp.bfloat16)
    query_grad, kv_part, bucket_rows = attend_back(
        place, bias_table, projected_rows, key_values, attended_grad
    )
    kv_grad = lax.psum_scatter(kv_part, "seq", scatter_dimension=1, tiled=True)
    out_part = lax.dot_general(
        attended_low, branch_low, CONTRACT_ROWS, preferred_element_type=jnp.float32
    )
    expert_grad = lax.psum_scatter(
        jnp.concatenate([first_term, second_term], axis=1),
        ("dp", "seq"),
        scatter_dimension=0,
        tiled=True,
    ).astype(jnp.float32)
    w_in_grad = expert_grad[:, :FF][None]
    w_out_grad = expert_grad[:, FF:].T[None]
    projected_grad = jnp.concatenate([query_grad, kv_grad[0], kv_grad[1]], axis=1)
    qkv_part = lax.dot_general(
        normed_low, projected_grad, CONTRACT_ROWS, preferred_element_type=jnp.float32
    )
    router_part = jnp.pad(router_part, ((0, 0), (0, PAIR - experts_total)))
    weight_parts = jnp.concatenate([qkv_part, out_part, router_part], axis=1)
    weight_grads = lax.psum_scatter(
        weight_parts.astype(jnp.bfloat16), everywhere, scatter_dimension=0, tiled=True
    ).astype(jnp.float32)
    qkv_grad, out_grad = weight_grads[:, : 3 * D], weight_grads[:, 3 * D : 4 * D]
    router_grad = weight_grads[:, 4 * D : 4 * D + experts_total]
    normed_grad = jnp.einsum(
        "qe,de->qd", projected_grad, qkv_full, preferred_element_type=jnp.float32
    )
    input_norm_grad, gain_one = norm_backward(normed_grad, normal_one, inverse_one, norm_gains[0])
    input_grad = (middle_grad + input_norm_grad).astype(jnp.bfloat16)[None]
    gains_grad, table_grad = lax.psum(
        (jnp.stack([gain_one, gain_two]), jnp.sum(bucket_rows, axis=-1).T), everywhere
    )
    return (
        layer_out,
        input_grad,
        qkv_grad,
        out_grad,
        router_grad,
        w_in_grad,
        w_out_grad,
        gains_grad,
        table_grad,
    )


def solution(mesh):
    return jax.shard_map(
        local,
        mesh=mesh,
        in_specs=(
            P(("dp", "expert"), "seq", None),
            P(("dp", "seq", "expert"), None),
            P(("dp", "seq", "expert"), None),
            P(("dp", "seq", "expert"), None),
            P("expert", ("dp", "seq"), None),
            P("expert", None, ("dp", "seq")),
            P(),
            P(),
            P(("dp", "expert"), "seq", None),
            P(("dp", "expert"), "seq", None),
        ),
        out_specs=(
            P(("dp", "expert"), "seq", None),
            P(("dp", "expert"), "seq", None),
            P(("dp", "seq", "expert"), None),
            P(("dp", "seq", "expert"), None),
            P(("dp", "seq", "expert"), None),
            P("expert", ("dp", "seq"), None),
            P("expert", None, ("dp", "seq")),
            P(),
            P(),
        ),
        check_vma=False,
    )
```

```python
import functools
import math

import jax
import jax.numpy as jnp
from jax import lax
from jax.experimental import pallas as pl
from jax.experimental.pallas import tpu as pltpu
from jax.sharding import PartitionSpec as P

D = 768
HEADS = 12
HEAD_DIM = 64
FF = 3072
BUCKETS = 32
LEN_DEV = 256


EPS = 1e-06
HIGH_PRECISION = lax.Precision.HIGHEST
CONTRACT_ROWS = (((0,), (0,)), ((), ()))


def bucket_edges(bucket_count):
    exact_count = bucket_count // 2
    boundaries = list(range(1, exact_count + 1))
    for bucket_index in range(exact_count + 1, bucket_count):
        power = (bucket_index - exact_count) / (bucket_count - exact_count)
        boundaries.append(math.ceil(exact_count * (128.0 / exact_count) ** power))
    return boundaries


def bucket_ids(distance, bucket_count):
    distance = jnp.maximum(distance, 0)
    bucket_sum = jnp.zeros(distance.shape, jnp.int32)
    for boundary in bucket_edges(bucket_count):
        bucket_sum = bucket_sum + (distance >= boundary).astype(jnp.int32)
    return bucket_sum


def norm_forward(values, scale_gain):
    inverse = lax.rsqrt(jnp.mean(values * values, axis=-1, keepdims=True) + EPS)
    normal_rows = values * inverse
    return (normal_rows * scale_gain, normal_rows, inverse)


def norm_backward(grad_out, normal_rows, inverse, scale_gain):
    gain_part = jnp.sum(grad_out * normal_rows, axis=0)
    scaled = grad_out * scale_gain
    value_grad = inverse * (
        scaled - normal_rows * jnp.mean(scaled * normal_rows, axis=-1, keepdims=True)
    )
    return (value_grad, gain_part)


def to_slots(slot_table, rows):
    return jnp.dot(slot_table, rows, preferred_element_type=jnp.float32).astype(jnp.bfloat16)


def from_slots(slot_table, rows):
    return lax.dot_general(slot_table, rows, CONTRACT_ROWS, preferred_element_type=jnp.float32)


TILE = 128
PAIR = 128
MASKED = -1e30
MATMUL_NT = (((1,), (1,)), ((), ()))


def matmul(left, right, dims=(((1,), (0,)), ((), ()))):
    return lax.dot_general(left, right, dims, preferred_element_type=jnp.float32)


def band_distance():
    key_row = lax.broadcasted_iota(jnp.int32, (2 * TILE, TILE), 0)
    query_column = lax.broadcasted_iota(jnp.int32, (2 * TILE, TILE), 1)
    return TILE + query_column - key_row


def fill_bias(strip, table_ref, head, tiles):
    distance = band_distance()
    band = jnp.full((2 * TILE, TILE), table_ref[0, head], jnp.float32)
    for bucket, edge in enumerate(bucket_edges(BUCKETS)):
        band = jnp.where(distance >= edge, table_ref[bucket + 1, head], band)
    band = jnp.where(distance >= 0, band, MASKED)
    far = (tiles - 2) * TILE
    strip[0:far, :] = jnp.full((far, TILE), table_ref[BUCKETS - 1, head], jnp.float32)
    strip[far : far + 2 * TILE, :] = band


def head_probabilities(strip, place, queries, keys, tiles):
    scores = matmul(keys, queries, MATMUL_NT)
    columns = []
    for part in range(LEN_DEV // TILE):
        blocks = []
        for slot in range(tiles * TILE // LEN_DEV):
            owner = jnp.bitwise_xor(place, slot)
            start = (tiles - 1 - part) * TILE + (owner - place) * LEN_DEV
            blocks.append(strip[pl.ds(pl.multiple_of(start, TILE), LEN_DEV), :])
        columns.append(jnp.concatenate(blocks, axis=0))
    scores = scores + jnp.concatenate(columns, axis=1)
    exps = jnp.exp(scores - jnp.max(scores, axis=0, keepdims=True))
    return exps * (1.0 / jnp.sum(exps, axis=0, keepdims=True))


def lane_halves(shape):
    return lax.broadcasted_iota(jnp.int32, shape, 1) < HEAD_DIM


def attend_kernel(tiles, place_ref, table_ref, q_ref, k_ref, v_ref, out_ref, strip):
    pair = pl.program_id(0)
    place = place_ref[0]

    @pl.when(pair == 0)
    def _():
        strip[tiles * TILE :, :] = jnp.full(((tiles - 1) * TILE, TILE), MASKED, jnp.float32)

    keys, values = k_ref[...], v_ref[...]
    queries = q_ref[...] * jnp.bfloat16(HEAD_DIM**-0.5)
    first = lane_halves(queries.shape)
    zero = jnp.zeros_like(queries)
    results = []
    for half in range(2):
        fill_bias(strip, table_ref, pair * 2 + half, tiles)
        own = jnp.where(first, queries, zero) if half == 0 else jnp.where(first, zero, queries)
        probs = head_probabilities(strip, place, own, keys, tiles).astype(jnp.bfloat16)
        results.append(matmul(values, probs, CONTRACT_ROWS))
    top = lax.broadcasted_iota(jnp.int32, results[0].shape, 0) < HEAD_DIM
    out_ref[...] = jnp.where(top, results[0], results[1]).T.astype(out_ref.dtype)


def attend_back_kernel(
    tiles, place_ref, table_ref, q_ref, k_ref, v_ref, g_ref, dq_ref, dkv_ref, sums_ref, strip, held
):
    pair = pl.program_id(0)
    place = place_ref[0]

    @pl.when(pair == 0)
    def _():
        strip[tiles * TILE :, :] = jnp.full(((tiles - 1) * TILE, TILE), MASKED, jnp.float32)

    keys, values = k_ref[...], v_ref[...]
    queries = q_ref[...] * jnp.bfloat16(HEAD_DIM**-0.5)
    grads = g_ref[...]
    first = lane_halves(queries.shape)
    zero = jnp.zeros_like(queries)
    distance = band_distance()
    buckets = jnp.full(distance.shape, -1, jnp.int32)
    for bucket, edge in enumerate([0] + bucket_edges(BUCKETS)):
        buckets = jnp.where(distance >= edge, bucket, buckets)
    q_parts, k_parts, v_parts = [], [], []
    for half in range(2):
        fill_bias(strip, table_ref, pair * 2 + half, tiles)
        own = jnp.where(first, queries, zero) if half == 0 else jnp.where(first, zero, queries)
        own_grads = jnp.where(first, grads, zero) if half == 0 else jnp.where(first, zero, grads)
        probs = head_probabilities(strip, place, own, keys, tiles)
        prob_grad = matmul(values, own_grads, MATMUL_NT)
        dots = jnp.sum(probs * prob_grad, axis=0, keepdims=True)
        score_grad = (probs * (prob_grad - dots)).astype(jnp.bfloat16)
        held[...] = score_grad
        k_parts.append(matmul(score_grad, queries))
        v_parts.append(matmul(probs.astype(jnp.bfloat16), grads))
        q_parts.append(matmul(keys, score_grad, CONTRACT_ROWS))
        band = jnp.zeros((2 * TILE, TILE), jnp.float32)
        for part in range(LEN_DEV // TILE):
            cols = slice(part * TILE, (part + 1) * TILE)
            same = score_grad[part * TILE : (part + 1) * TILE, cols].astype(jnp.float32)
            if part > 0:
                near = score_grad[(part - 1) * TILE : part * TILE, cols].astype(jnp.float32)
            else:
                slot = jnp.bitwise_xor(place, jnp.maximum(place - 1, 0))
                start = (slot + 1) * LEN_DEV - TILE
                near = held[pl.ds(pl.multiple_of(start, TILE), TILE), cols].astype(jnp.float32)
                near = jnp.where(place > 0, near, 0.0)
            band = band + jnp.concatenate([near, same], axis=0)
        total = jnp.sum(score_grad.astype(jnp.float32), axis=0, keepdims=True)
        total = total[:, :TILE] + total[:, TILE:]
        far = total - jnp.sum(band, axis=0, keepdims=True)
        for bucket in range(BUCKETS):
            row = jnp.sum(jnp.where(buckets == bucket, band, 0.0), axis=0, keepdims=True)
            if bucket == BUCKETS - 1:
                row = row + far
            sums_ref[half, bucket : bucket + 1, :] = row
    top = lax.broadcasted_iota(jnp.int32, q_parts[0].shape, 0) < HEAD_DIM
    dq = jnp.where(top, q_parts[0], q_parts[1]).T * HEAD_DIM**-0.5
    dq_ref[...] = dq.astype(dq_ref.dtype)
    side = lane_halves(k_parts[0].shape)
    for index, parts in enumerate((k_parts, v_parts)):
        both = jnp.where(side, parts[0], parts[1]).astype(dkv_ref.dtype)
        for slot in range(dkv_ref.shape[0]):
            dkv_ref[slot, index] = both[slot * LEN_DEV : (slot + 1) * LEN_DEV]


def attention_specs(full_length):
    pairs = D // PAIR
    smem = pl.BlockSpec(memory_space=pltpu.SMEM)
    rows = pl.BlockSpec((LEN_DEV, PAIR), lambda pair: (0, pair))
    keys = pl.BlockSpec((full_length, PAIR), lambda pair: (0, pair))
    values = pl.BlockSpec((full_length, PAIR), lambda pair: (0, pair + pairs))
    return pairs, smem, rows, keys, values


def attend(place, bias_table, projected, key_values):
    full_length = key_values.shape[0]
    tiles = full_length // TILE
    pairs, smem, rows, keys, values = attention_specs(full_length)
    return pl.pallas_call(
        functools.partial(attend_kernel, tiles),
        grid=(pairs,),
        out_shape=jax.ShapeDtypeStruct((LEN_DEV, D), jnp.bfloat16),
        in_specs=[smem, smem, rows, keys, values],
        out_specs=rows,
        scratch_shapes=[pltpu.VMEM(((2 * tiles - 1) * TILE, TILE), jnp.float32)],
        compiler_params=pltpu.CompilerParams(vmem_limit_bytes=40 * 2**20),
        cost_estimate=pl.CostEstimate(
            flops=4 * LEN_DEV * full_length * PAIR * HEADS,
            bytes_accessed=2 * D * (2 * LEN_DEV + 2 * full_length),
            transcendentals=HEADS * LEN_DEV * full_length,
        ),
    )(place, bias_table, projected, key_values, key_values)


def attend_back(place, bias_table, projected, key_values, attended_grad):
    full_length = key_values.shape[0]
    tiles = full_length // TILE
    pairs, smem, rows, keys, values = attention_specs(full_length)
    return pl.pallas_call(
        functools.partial(attend_back_kernel, tiles),
        grid=(pairs,),
        out_shape=(
            jax.ShapeDtypeStruct((LEN_DEV, D), jnp.bfloat16),
            jax.ShapeDtypeStruct((full_length // LEN_DEV, 2, LEN_DEV, D), jnp.bfloat16),
            jax.ShapeDtypeStruct((HEADS, BUCKETS, TILE), jnp.float32),
        ),
        in_specs=[smem, smem, rows, keys, values, rows],
        out_specs=(
            rows,
            pl.BlockSpec(
                (full_length // LEN_DEV, 2, LEN_DEV, PAIR), lambda pair: (0, 0, 0, pair)
            ),
            pl.BlockSpec((2, BUCKETS, TILE), lambda pair: (pair, 0, 0)),
        ),
        scratch_shapes=[
            pltpu.VMEM(((2 * tiles - 1) * TILE, TILE), jnp.float32),
            pltpu.VMEM((full_length, LEN_DEV), jnp.bfloat16),
        ],
        compiler_params=pltpu.CompilerParams(vmem_limit_bytes=48 * 2**20),
        cost_estimate=pl.CostEstimate(
            flops=10 * LEN_DEV * full_length * PAIR * HEADS,
            bytes_accessed=2 * D * (3 * LEN_DEV + 4 * full_length),
            transcendentals=HEADS * LEN_DEV * full_length,
        ),
    )(place, bias_table, projected, key_values, key_values, attended_grad)


def swap_pairs(block, bit):
    pairs = [(index, index ^ bit) for index in range(lax.axis_size("seq"))]
    return lax.ppermute(block, "seq", pairs)


def spread_sequence(block):
    held = {0: block}
    bit = lax.axis_size("seq") // 2
    while bit:
        held.update({slot ^ bit: swap_pairs(held[slot], bit) for slot in list(held)})
        bit //= 2
    return [held[slot] for slot in range(len(held))]


def sum_sequence(parts):
    held = {slot: parts[slot] for slot in range(parts.shape[0])}
    bit = 1
    while bit < parts.shape[0]:
        kept = {}
        for slot in held:
            if not slot & bit:
                arrived = swap_pairs(held[slot ^ bit].astype(jnp.bfloat16), bit)
                kept[slot] = held[slot].astype(jnp.float32) + arrived.astype(jnp.float32)
        held = kept
        bit *= 2
    return held[0].astype(jnp.bfloat16)


def swap_experts(slots, experts_total):
    return lax.all_to_all(
        slots.reshape(experts_total, slots.shape[0] // experts_total, slots.shape[1]),
        "expert",
        split_axis=0,
        concat_axis=0,
        tiled=True,
    ).reshape(slots.shape)


def local(
    tokens,
    qkv_weight,
    out_weight,
    router_weight,
    w_in,
    w_out,
    norm_gains,
    bias_table,
    expert_ids,
    cotangent,
):
    everywhere = ("dp", "seq", "expert")
    inputs = tokens[0].astype(jnp.float32)
    experts_total = lax.axis_size("expert")
    capacity = 3 * LEN_DEV // experts_total
    router_pad = jnp.zeros((router_weight.shape[0], PAIR - experts_total), jnp.bfloat16)
    packed = jnp.concatenate([qkv_weight, out_weight, router_weight, router_pad], axis=1)
    packed = lax.all_gather(packed, "expert", axis=0, tiled=True)
    packed = lax.all_gather(packed, ("dp", "seq"), axis=0, tiled=True)
    qkv_full, out_full = packed[:, : 3 * D], packed[:, 3 * D : 4 * D]
    router_full = packed[:, 4 * D : 4 * D + experts_total]

    route_ids = expert_ids[0]
    expert_names = jnp.arange(experts_total, dtype=jnp.int32)
    choose = (route_ids[..., None] == expert_names).astype(jnp.float32)
    flat_ids = route_ids.reshape(-1)
    expert_hits = (flat_ids[:, None] == expert_names).astype(jnp.int32)
    slot_rank = jnp.sum((jnp.cumsum(expert_hits, axis=0) - 1) * expert_hits, axis=-1)
    places = (flat_ids * capacity + slot_rank).reshape(LEN_DEV, 2)
    slot_index = jnp.arange(experts_total * capacity, dtype=jnp.int32)[:, None]
    hits = [slot_index == places[None, :, k] for k in range(2)]
    tables = [hit.astype(jnp.bfloat16) for hit in hits]
    token_table = (hits[0] | hits[1]).astype(jnp.bfloat16)
    arrived_cotangent = swap_experts(to_slots(token_table, cotangent[0]), experts_total)

    normalized_rows, normal_one, inverse_one = norm_forward(inputs, norm_gains[0])
    normed_low = normalized_rows.astype(jnp.bfloat16)
    normed_low, arrived_cotangent = lax.optimization_barrier((normed_low, arrived_cotangent))
    projected_rows = jnp.dot(normed_low, qkv_full, preferred_element_type=jnp.float32).astype(
        jnp.bfloat16
    )
    key_values = jnp.concatenate(spread_sequence(projected_rows[:, D:]), axis=0)
    place = lax.axis_index("seq").astype(jnp.int32).reshape(1)
    attended_low = attend(place, bias_table, projected_rows, key_values)
    w_in_full = lax.all_gather(w_in, ("dp", "seq"), axis=1, tiled=True)[0]
    w_out_full = lax.all_gather(w_out, ("dp", "seq"), axis=2, tiled=True)[0]
    middle = inputs + jnp.dot(attended_low, out_full, preferred_element_type=jnp.float32)
    mixed, normal_two, inverse_two = norm_forward(middle, norm_gains[1])
    mixed_low = mixed.astype(jnp.bfloat16)
    expert_rows = swap_experts(to_slots(token_table, mixed_low), experts_total)
    router_logits = jnp.dot(mixed_low, router_full, preferred_element_type=jnp.float32)
    chosen = jnp.sum(choose * router_logits[:, None, :], axis=-1)
    gate_weights = jax.nn.softmax(chosen, axis=-1)
    gate_slots = jnp.sum(
        jnp.where(hits[0], gate_weights[None, :, 0], 0.0)
        + jnp.where(hits[1], gate_weights[None, :, 1], 0.0),
        axis=1,
    )
    arrived_gates = lax.all_to_all(
        gate_slots.reshape(experts_total, capacity),
        "expert",
        split_axis=0,
        concat_axis=0,
        tiled=True,
    ).reshape(-1, 1)
    pre_act = jnp.dot(expert_rows, w_in_full, preferred_element_type=jnp.float32)
    hidden_low = jax.nn.gelu(pre_act).astype(jnp.bfloat16)
    expert_out = jnp.dot(hidden_low, w_out_full, preferred_element_type=jnp.float32).astype(
        jnp.bfloat16
    )
    returned = swap_experts(expert_out, experts_total)
    arrived_grad = (arrived_gates * arrived_cotangent.astype(jnp.float32)).astype(jnp.bfloat16)
    hidden_grad = jnp.einsum(
        "rd,fd->rf", arrived_grad, w_out_full, preferred_element_type=jnp.float32
    )
    gelu_value, gelu_pull = jax.vjp(jax.nn.gelu, pre_act)
    pre_grad = gelu_pull(hidden_grad)[0].astype(jnp.bfloat16)
    row_grad = jnp.einsum(
        "rf,df->rd", pre_grad, w_in_full, preferred_element_type=jnp.float32
    ).astype(jnp.bfloat16)
    returned_grad = swap_experts(row_grad, experts_total)
    first_term = lax.dot_general(
        expert_rows, pre_grad, CONTRACT_ROWS, preferred_element_type=jnp.float32
    ).astype(jnp.bfloat16)
    second_term = lax.dot_general(
        arrived_grad, hidden_low, CONTRACT_ROWS, preferred_element_type=jnp.float32
    ).astype(jnp.bfloat16)

    returned, first_term, second_term = lax.optimization_barrier(
        (returned, first_term, second_term)
    )
    upstream = cotangent[0].astype(jnp.float32)
    gathered = [from_slots(table, returned) for table in tables]
    block_out = middle + gate_weights[:, :1] * gathered[0] + gate_weights[:, 1:] * gathered[1]
    layer_out = block_out.astype(jnp.bfloat16)[None]
    gate_grad = jnp.stack([jnp.sum(upstream * rows, axis=-1) for rows in gathered], axis=-1)
    gate_mean = jnp.sum(gate_weights * gate_grad, axis=-1, keepdims=True)
    chosen_grad = gate_weights * (gate_grad - gate_mean)
    logit_grad = jnp.sum(choose * chosen_grad[..., None], axis=1)
    router_part = lax.dot_general(
        mixed_low.astype(jnp.float32), logit_grad, CONTRACT_ROWS, precision=HIGH_PRECISION
    )
    copy_back = from_slots(token_table, returned_grad)
    mixed_grad = copy_back + jnp.dot(
        logit_grad, router_full.astype(jnp.float32).T, precision=HIGH_PRECISION
    )
    middle_norm_grad, gain_two = norm_backward(mixed_grad, normal_two, inverse_two, norm_gains[1])
    middle_grad = upstream + middle_norm_grad
    branch_low = middle_grad.astype(jnp.bfloat16)
    attended_grad = jnp.einsum(
        "qe,de->qd", branch_low, out_full, preferred_element_type=jnp.float32
    ).astype(jnp.bfloat16)
    query_grad, kv_part, bucket_rows = attend_back(
        place, bias_table, projected_rows, key_values, attended_grad
    )
    kv_grad = sum_sequence(kv_part)
    out_part = lax.dot_general(
        attended_low, branch_low, CONTRACT_ROWS, preferred_element_type=jnp.float32
    )
    first_sum, second_sum = [
        lax.psum_scatter(term, ("dp", "seq"), scatter_dimension=0, tiled=True)
        for term in (first_term, second_term)
    ]
    projected_grad = jnp.concatenate([query_grad, kv_grad[0], kv_grad[1]], axis=1)
    projected_grad, first_sum, second_sum = lax.optimization_barrier(
        (projected_grad, first_sum, second_sum)
    )
    w_in_grad = first_sum.astype(jnp.float32)[None]
    w_out_grad = second_sum.astype(jnp.float32).T[None]
    qkv_part = lax.dot_general(
        normed_low, projected_grad, CONTRACT_ROWS, preferred_element_type=jnp.float32
    )
    router_part = jnp.pad(router_part, ((0, 0), (0, PAIR - experts_total)))
    weight_parts = jnp.concatenate([qkv_part, out_part, router_part], axis=1)
    weight_grads = lax.psum_scatter(
        weight_parts.astype(jnp.bfloat16), ("dp", "seq"), scatter_dimension=0, tiled=True
    )
    weight_grads = lax.psum_scatter(
        weight_grads, "expert", scatter_dimension=0, tiled=True
    ).astype(jnp.float32)
    qkv_grad, out_grad = weight_grads[:, : 3 * D], weight_grads[:, 3 * D : 4 * D]
    router_grad = weight_grads[:, 4 * D : 4 * D + experts_total]
    normed_grad = jnp.einsum(
        "qe,de->qd", projected_grad, qkv_full, preferred_element_type=jnp.float32
    )
    input_norm_grad, gain_one = norm_backward(normed_grad, normal_one, inverse_one, norm_gains[0])
    input_grad = (middle_grad + input_norm_grad).astype(jnp.bfloat16)[None]
    gains_grad, table_grad = lax.psum(
        (jnp.stack([gain_one, gain_two]), jnp.sum(bucket_rows, axis=-1).T), everywhere
    )
    return (
        layer_out,
        input_grad,
        qkv_grad,
        out_grad,
        router_grad,
        w_in_grad,
        w_out_grad,
        gains_grad,
        table_grad,
    )


def solution(mesh):
    return jax.shard_map(
        local,
        mesh=mesh,
        in_specs=(
            P(("dp", "expert"), "seq", None),
            P(("dp", "seq", "expert"), None),
            P(("dp", "seq", "expert"), None),
            P(("dp", "seq", "expert"), None),
            P("expert", ("dp", "seq"), None),
            P("expert", None, ("dp", "seq")),
            P(),
            P(),
            P(("dp", "expert"), "seq", None),
            P(("dp", "expert"), "seq", None),
        ),
        out_specs=(
            P(("dp", "expert"), "seq", None),
            P(("dp", "expert"), "seq", None),
            P(("dp", "seq", "expert"), None),
            P(("dp", "seq", "expert"), None),
            P(("dp", "seq", "expert"), None),
            P("expert", ("dp", "seq"), None),
            P("expert", None, ("dp", "seq")),
            P(),
            P(),
        ),
        check_vma=False,
    )
```

```python
import functools
import math

import jax
import jax.numpy as jnp
from jax import lax
from jax.experimental import pallas as pl
from jax.experimental.pallas import tpu as pltpu
from jax.sharding import PartitionSpec as P

D = 768
HEADS = 12
HEAD_DIM = 64
FF = 3072
BUCKETS = 32
LEN_DEV = 256


EPS = 1e-06
HIGH_PRECISION = lax.Precision.HIGHEST
CONTRACT_ROWS = (((0,), (0,)), ((), ()))


def bucket_edges(bucket_count):
    exact_count = bucket_count // 2
    boundaries = list(range(1, exact_count + 1))
    for bucket_index in range(exact_count + 1, bucket_count):
        power = (bucket_index - exact_count) / (bucket_count - exact_count)
        boundaries.append(math.ceil(exact_count * (128.0 / exact_count) ** power))
    return boundaries


def bucket_ids(distance, bucket_count):
    distance = jnp.maximum(distance, 0)
    bucket_sum = jnp.zeros(distance.shape, jnp.int32)
    for boundary in bucket_edges(bucket_count):
        bucket_sum = bucket_sum + (distance >= boundary).astype(jnp.int32)
    return bucket_sum


def norm_forward(values, scale_gain):
    inverse = lax.rsqrt(jnp.mean(values * values, axis=-1, keepdims=True) + EPS)
    normal_rows = values * inverse
    return (normal_rows * scale_gain, normal_rows, inverse)


def norm_backward(grad_out, normal_rows, inverse, scale_gain):
    gain_part = jnp.sum(grad_out * normal_rows, axis=0)
    scaled = grad_out * scale_gain
    value_grad = inverse * (
        scaled - normal_rows * jnp.mean(scaled * normal_rows, axis=-1, keepdims=True)
    )
    return (value_grad, gain_part)


def to_slots(slot_table, rows):
    return jnp.dot(slot_table, rows, preferred_element_type=jnp.float32).astype(jnp.bfloat16)


def from_slots(slot_table, rows):
    return lax.dot_general(slot_table, rows, CONTRACT_ROWS, preferred_element_type=jnp.float32)


TILE = 128
PAIR = 128
MASKED = -1e30
MATMUL_NT = (((1,), (1,)), ((), ()))


def matmul(left, right, dims=(((1,), (0,)), ((), ()))):
    return lax.dot_general(left, right, dims, preferred_element_type=jnp.float32)


def band_distance():
    key_row = lax.broadcasted_iota(jnp.int32, (2 * TILE, TILE), 0)
    query_column = lax.broadcasted_iota(jnp.int32, (2 * TILE, TILE), 1)
    return TILE + query_column - key_row


def fill_bias(strip, table_ref, head, tiles):
    distance = band_distance()
    band = jnp.full((2 * TILE, TILE), table_ref[0, head], jnp.float32)
    for bucket, edge in enumerate(bucket_edges(BUCKETS)):
        band = jnp.where(distance >= edge, table_ref[bucket + 1, head], band)
    band = jnp.where(distance >= 0, band, MASKED)
    far = (tiles - 2) * TILE
    strip[0:far, :] = jnp.full((far, TILE), table_ref[BUCKETS - 1, head], jnp.float32)
    strip[far : far + 2 * TILE, :] = band


def head_probabilities(strip, place, queries, keys, tiles):
    scores = matmul(keys, queries, MATMUL_NT)
    columns = []
    for part in range(LEN_DEV // TILE):
        blocks = []
        for slot in range(tiles * TILE // LEN_DEV):
            owner = jnp.bitwise_xor(place, slot)
            start = (tiles - 1 - part) * TILE + (owner - place) * LEN_DEV
            blocks.append(strip[pl.ds(pl.multiple_of(start, TILE), LEN_DEV), :])
        columns.append(jnp.concatenate(blocks, axis=0))
    scores = scores + jnp.concatenate(columns, axis=1)
    exps = jnp.exp(scores - jnp.max(scores, axis=0, keepdims=True))
    return exps * (1.0 / jnp.sum(exps, axis=0, keepdims=True))


def lane_halves(shape):
    return lax.broadcasted_iota(jnp.int32, shape, 1) < HEAD_DIM


def attend_kernel(tiles, place_ref, table_ref, q_ref, k_ref, v_ref, out_ref, strip):
    pair = pl.program_id(0)
    place = place_ref[0]

    @pl.when(pair == 0)
    def _():
        strip[tiles * TILE :, :] = jnp.full(((tiles - 1) * TILE, TILE), MASKED, jnp.float32)

    keys, values = k_ref[...], v_ref[...]
    queries = q_ref[...] * jnp.bfloat16(HEAD_DIM**-0.5)
    first = lane_halves(queries.shape)
    zero = jnp.zeros_like(queries)
    results = []
    for half in range(2):
        fill_bias(strip, table_ref, pair * 2 + half, tiles)
        own = jnp.where(first, queries, zero) if half == 0 else jnp.where(first, zero, queries)
        probs = head_probabilities(strip, place, own, keys, tiles).astype(jnp.bfloat16)
        results.append(matmul(values, probs, CONTRACT_ROWS))
    top = lax.broadcasted_iota(jnp.int32, results[0].shape, 0) < HEAD_DIM
    out_ref[...] = jnp.where(top, results[0], results[1]).T.astype(out_ref.dtype)


def attend_back_kernel(
    tiles, place_ref, table_ref, q_ref, k_ref, v_ref, g_ref, dq_ref, dkv_ref, sums_ref, strip, held
):
    pair = pl.program_id(0)
    place = place_ref[0]

    @pl.when(pair == 0)
    def _():
        strip[tiles * TILE :, :] = jnp.full(((tiles - 1) * TILE, TILE), MASKED, jnp.float32)

    keys, values = k_ref[...], v_ref[...]
    queries = q_ref[...] * jnp.bfloat16(HEAD_DIM**-0.5)
    grads = g_ref[...]
    first = lane_halves(queries.shape)
    zero = jnp.zeros_like(queries)
    distance = band_distance()
    buckets = jnp.full(distance.shape, -1, jnp.int32)
    for bucket, edge in enumerate([0] + bucket_edges(BUCKETS)):
        buckets = jnp.where(distance >= edge, bucket, buckets)
    q_parts, k_parts, v_parts = [], [], []
    for half in range(2):
        fill_bias(strip, table_ref, pair * 2 + half, tiles)
        own = jnp.where(first, queries, zero) if half == 0 else jnp.where(first, zero, queries)
        own_grads = jnp.where(first, grads, zero) if half == 0 else jnp.where(first, zero, grads)
        probs = head_probabilities(strip, place, own, keys, tiles)
        prob_grad = matmul(values, own_grads, MATMUL_NT)
        dots = jnp.sum(probs * prob_grad, axis=0, keepdims=True)
        score_grad = (probs * (prob_grad - dots)).astype(jnp.bfloat16)
        held[...] = score_grad
        k_parts.append(matmul(score_grad, queries))
        v_parts.append(matmul(probs.astype(jnp.bfloat16), grads))
        q_parts.append(matmul(keys, score_grad, CONTRACT_ROWS))
        band = jnp.zeros((2 * TILE, TILE), jnp.float32)
        for part in range(LEN_DEV // TILE):
            cols = slice(part * TILE, (part + 1) * TILE)
            same = score_grad[part * TILE : (part + 1) * TILE, cols].astype(jnp.float32)
            if part > 0:
                near = score_grad[(part - 1) * TILE : part * TILE, cols].astype(jnp.float32)
            else:
                slot = jnp.bitwise_xor(place, jnp.maximum(place - 1, 0))
                start = (slot + 1) * LEN_DEV - TILE
                near = held[pl.ds(pl.multiple_of(start, TILE), TILE), cols].astype(jnp.float32)
                near = jnp.where(place > 0, near, 0.0)
            band = band + jnp.concatenate([near, same], axis=0)
        total = jnp.sum(score_grad.astype(jnp.float32), axis=0, keepdims=True)
        total = total[:, :TILE] + total[:, TILE:]
        far = total - jnp.sum(band, axis=0, keepdims=True)
        for bucket in range(BUCKETS):
            row = jnp.sum(jnp.where(buckets == bucket, band, 0.0), axis=0, keepdims=True)
            if bucket == BUCKETS - 1:
                row = row + far
            sums_ref[half, bucket : bucket + 1, :] = row
    top = lax.broadcasted_iota(jnp.int32, q_parts[0].shape, 0) < HEAD_DIM
    dq = jnp.where(top, q_parts[0], q_parts[1]).T * HEAD_DIM**-0.5
    dq_ref[...] = dq.astype(dq_ref.dtype)
    side = lane_halves(k_parts[0].shape)
    for index, parts in enumerate((k_parts, v_parts)):
        both = jnp.where(side, parts[0], parts[1]).astype(dkv_ref.dtype)
        for slot in range(dkv_ref.shape[0]):
            dkv_ref[slot, index] = both[slot * LEN_DEV : (slot + 1) * LEN_DEV]


def attention_specs(full_length):
    pairs = D // PAIR
    smem = pl.BlockSpec(memory_space=pltpu.SMEM)
    rows = pl.BlockSpec((LEN_DEV, PAIR), lambda pair: (0, pair))
    keys = pl.BlockSpec((full_length, PAIR), lambda pair: (0, pair))
    values = pl.BlockSpec((full_length, PAIR), lambda pair: (0, pair + pairs))
    return pairs, smem, rows, keys, values


def attend(place, bias_table, projected, key_values):
    full_length = key_values.shape[0]
    tiles = full_length // TILE
    pairs, smem, rows, keys, values = attention_specs(full_length)
    return pl.pallas_call(
        functools.partial(attend_kernel, tiles),
        grid=(pairs,),
        out_shape=jax.ShapeDtypeStruct((LEN_DEV, D), jnp.bfloat16),
        in_specs=[smem, smem, rows, keys, values],
        out_specs=rows,
        scratch_shapes=[pltpu.VMEM(((2 * tiles - 1) * TILE, TILE), jnp.float32)],
        compiler_params=pltpu.CompilerParams(vmem_limit_bytes=40 * 2**20),
        cost_estimate=pl.CostEstimate(
            flops=4 * LEN_DEV * full_length * PAIR * HEADS,
            bytes_accessed=2 * D * (2 * LEN_DEV + 2 * full_length),
            transcendentals=HEADS * LEN_DEV * full_length,
        ),
    )(place, bias_table, projected, key_values, key_values)


def attend_back(place, bias_table, projected, key_values, attended_grad):
    full_length = key_values.shape[0]
    tiles = full_length // TILE
    pairs, smem, rows, keys, values = attention_specs(full_length)
    return pl.pallas_call(
        functools.partial(attend_back_kernel, tiles),
        grid=(pairs,),
        out_shape=(
            jax.ShapeDtypeStruct((LEN_DEV, D), jnp.bfloat16),
            jax.ShapeDtypeStruct((full_length // LEN_DEV, 2, LEN_DEV, D), jnp.bfloat16),
            jax.ShapeDtypeStruct((HEADS, BUCKETS, TILE), jnp.float32),
        ),
        in_specs=[smem, smem, rows, keys, values, rows],
        out_specs=(
            rows,
            pl.BlockSpec(
                (full_length // LEN_DEV, 2, LEN_DEV, PAIR), lambda pair: (0, 0, 0, pair)
            ),
            pl.BlockSpec((2, BUCKETS, TILE), lambda pair: (pair, 0, 0)),
        ),
        scratch_shapes=[
            pltpu.VMEM(((2 * tiles - 1) * TILE, TILE), jnp.float32),
            pltpu.VMEM((full_length, LEN_DEV), jnp.bfloat16),
        ],
        compiler_params=pltpu.CompilerParams(vmem_limit_bytes=48 * 2**20),
        cost_estimate=pl.CostEstimate(
            flops=10 * LEN_DEV * full_length * PAIR * HEADS,
            bytes_accessed=2 * D * (3 * LEN_DEV + 4 * full_length),
            transcendentals=HEADS * LEN_DEV * full_length,
        ),
    )(place, bias_table, projected, key_values, key_values, attended_grad)


def swap_pairs(block, bit):
    pairs = [(index, index ^ bit) for index in range(lax.axis_size("seq"))]
    return lax.ppermute(block, "seq", pairs)


def spread_sequence(block):
    held = {0: block}
    bit = lax.axis_size("seq") // 2
    while bit:
        held.update({slot ^ bit: swap_pairs(held[slot], bit) for slot in list(held)})
        bit //= 2
    return [held[slot] for slot in range(len(held))]


def sum_sequence(parts):
    held = {slot: parts[slot] for slot in range(parts.shape[0])}
    bit = 1
    while bit < parts.shape[0]:
        kept = {}
        for slot in held:
            if not slot & bit:
                arrived = swap_pairs(held[slot ^ bit].astype(jnp.bfloat16), bit)
                kept[slot] = held[slot].astype(jnp.float32) + arrived.astype(jnp.float32)
        held = kept
        bit *= 2
    return held[0].astype(jnp.bfloat16)


def swap_experts(slots, experts_total):
    return lax.all_to_all(
        slots.reshape(experts_total, slots.shape[0] // experts_total, slots.shape[1]),
        "expert",
        split_axis=0,
        concat_axis=0,
        tiled=True,
    ).reshape(slots.shape)


def local(
    tokens,
    qkv_weight,
    out_weight,
    router_weight,
    w_in,
    w_out,
    norm_gains,
    bias_table,
    expert_ids,
    cotangent,
):
    everywhere = ("dp", "seq", "expert")
    inputs = tokens[0].astype(jnp.float32)
    experts_total = lax.axis_size("expert")
    capacity = 3 * LEN_DEV // experts_total
    router_pad = jnp.zeros((router_weight.shape[0], PAIR - experts_total), jnp.bfloat16)
    packed = jnp.concatenate([qkv_weight, out_weight, router_weight, router_pad], axis=1)
    packed = lax.all_gather(packed, "expert", axis=0, tiled=True)
    packed = lax.all_gather(packed, ("dp", "seq"), axis=0, tiled=True)
    qkv_full, out_full = packed[:, : 3 * D], packed[:, 3 * D : 4 * D]
    router_full = packed[:, 4 * D : 4 * D + experts_total]

    route_ids = expert_ids[0]
    expert_names = jnp.arange(experts_total, dtype=jnp.int32)
    choose = (route_ids[..., None] == expert_names).astype(jnp.float32)
    flat_ids = route_ids.reshape(-1)
    expert_hits = (flat_ids[:, None] == expert_names).astype(jnp.int32)
    slot_rank = jnp.sum((jnp.cumsum(expert_hits, axis=0) - 1) * expert_hits, axis=-1)
    places = (flat_ids * capacity + slot_rank).reshape(LEN_DEV, 2)
    slot_index = jnp.arange(experts_total * capacity, dtype=jnp.int32)[:, None]
    hits = [slot_index == places[None, :, k] for k in range(2)]
    tables = [hit.astype(jnp.bfloat16) for hit in hits]
    token_table = (hits[0] | hits[1]).astype(jnp.bfloat16)
    arrived_cotangent = swap_experts(to_slots(token_table, cotangent[0]), experts_total)

    normalized_rows, normal_one, inverse_one = norm_forward(inputs, norm_gains[0])
    normed_low = normalized_rows.astype(jnp.bfloat16)
    normed_low, arrived_cotangent = lax.optimization_barrier((normed_low, arrived_cotangent))
    projected_rows = jnp.dot(normed_low, qkv_full, preferred_element_type=jnp.float32).astype(
        jnp.bfloat16
    )
    key_values = jnp.concatenate(spread_sequence(projected_rows[:, D:]), axis=0)
    place = lax.axis_index("seq").astype(jnp.int32).reshape(1)
    attended_low = attend(place, bias_table, projected_rows, key_values)
    w_in_full = lax.all_gather(w_in, ("dp", "seq"), axis=1, tiled=True)[0]
    w_out_full = lax.all_gather(w_out, ("dp", "seq"), axis=2, tiled=True)[0]
    middle = inputs + jnp.dot(attended_low, out_full, preferred_element_type=jnp.float32)
    mixed, normal_two, inverse_two = norm_forward(middle, norm_gains[1])
    mixed_low = mixed.astype(jnp.bfloat16)
    expert_rows = swap_experts(to_slots(token_table, mixed_low), experts_total)
    router_logits = jnp.dot(mixed_low, router_full, preferred_element_type=jnp.float32)
    chosen = jnp.sum(choose * router_logits[:, None, :], axis=-1)
    gate_weights = jax.nn.softmax(chosen, axis=-1)
    gate_slots = jnp.sum(
        jnp.where(hits[0], gate_weights[None, :, 0], 0.0)
        + jnp.where(hits[1], gate_weights[None, :, 1], 0.0),
        axis=1,
    )
    gate_slots, expert_rows = lax.optimization_barrier((gate_slots, expert_rows))
    arrived_gates = lax.all_to_all(
        gate_slots.reshape(experts_total, capacity),
        "expert",
        split_axis=0,
        concat_axis=0,
        tiled=True,
    ).reshape(-1, 1)
    pre_act = jnp.dot(expert_rows, w_in_full, preferred_element_type=jnp.float32)
    hidden_low = jax.nn.gelu(pre_act).astype(jnp.bfloat16)
    expert_out = jnp.dot(hidden_low, w_out_full, preferred_element_type=jnp.float32).astype(
        jnp.bfloat16
    )
    returned = swap_experts(expert_out, experts_total)
    arrived_grad = (arrived_gates * arrived_cotangent.astype(jnp.float32)).astype(jnp.bfloat16)
    hidden_grad = jnp.einsum(
        "rd,fd->rf", arrived_grad, w_out_full, preferred_element_type=jnp.float32
    )
    gelu_value, gelu_pull = jax.vjp(jax.nn.gelu, pre_act)
    pre_grad = gelu_pull(hidden_grad)[0].astype(jnp.bfloat16)
    row_grad = jnp.einsum(
        "rf,df->rd", pre_grad, w_in_full, preferred_element_type=jnp.float32
    ).astype(jnp.bfloat16)
    row_grad, pre_grad, hidden_low = lax.optimization_barrier((row_grad, pre_grad, hidden_low))
    returned_grad = swap_experts(row_grad, experts_total)
    first_term = lax.dot_general(
        expert_rows, pre_grad, CONTRACT_ROWS, preferred_element_type=jnp.float32
    ).astype(jnp.bfloat16)
    second_term = lax.dot_general(
        arrived_grad, hidden_low, CONTRACT_ROWS, preferred_element_type=jnp.float32
    ).astype(jnp.bfloat16)

    expert_terms = jnp.concatenate([first_term, second_term], axis=1)
    returned, expert_terms = lax.optimization_barrier((returned, expert_terms))
    upstream = cotangent[0].astype(jnp.float32)
    gathered = [from_slots(table, returned) for table in tables]
    block_out = middle + gate_weights[:, :1] * gathered[0] + gate_weights[:, 1:] * gathered[1]
    layer_out = block_out.astype(jnp.bfloat16)[None]
    gate_grad = jnp.stack([jnp.sum(upstream * rows, axis=-1) for rows in gathered], axis=-1)
    gate_mean = jnp.sum(gate_weights * gate_grad, axis=-1, keepdims=True)
    chosen_grad = gate_weights * (gate_grad - gate_mean)
    logit_grad = jnp.sum(choose * chosen_grad[..., None], axis=1)
    router_part = lax.dot_general(
        mixed_low.astype(jnp.float32), logit_grad, CONTRACT_ROWS, precision=HIGH_PRECISION
    )
    copy_back = from_slots(token_table, returned_grad)
    mixed_grad = copy_back + jnp.dot(
        logit_grad, router_full.astype(jnp.float32).T, precision=HIGH_PRECISION
    )
    middle_norm_grad, gain_two = norm_backward(mixed_grad, normal_two, inverse_two, norm_gains[1])
    middle_grad = upstream + middle_norm_grad
    branch_low = middle_grad.astype(jnp.bfloat16)
    attended_grad = jnp.einsum(
        "qe,de->qd", branch_low, out_full, preferred_element_type=jnp.float32
    ).astype(jnp.bfloat16)
    query_grad, kv_part, bucket_rows = attend_back(
        place, bias_table, projected_rows, key_values, attended_grad
    )
    kv_grad = sum_sequence(kv_part)
    out_part = lax.dot_general(
        attended_low, branch_low, CONTRACT_ROWS, preferred_element_type=jnp.float32
    )
    expert_grad = lax.psum_scatter(
        expert_terms, ("dp", "seq"), scatter_dimension=0, tiled=True
    )
    projected_grad = jnp.concatenate([query_grad, kv_grad[0], kv_grad[1]], axis=1)
    projected_grad, expert_grad = lax.optimization_barrier((projected_grad, expert_grad))
    w_in_grad = expert_grad[:, :FF].astype(jnp.float32)[None]
    w_out_grad = expert_grad[:, FF:].astype(jnp.float32).T[None]
    qkv_part = lax.dot_general(
        normed_low, projected_grad, CONTRACT_ROWS, preferred_element_type=jnp.float32
    )
    router_part = jnp.pad(router_part, ((0, 0), (0, PAIR - experts_total)))
    weight_parts = jnp.concatenate([qkv_part, out_part, router_part], axis=1)
    weight_grads = lax.psum_scatter(
        weight_parts.astype(jnp.bfloat16), ("dp", "seq"), scatter_dimension=0, tiled=True
    )
    weight_grads = lax.psum_scatter(
        weight_grads, "expert", scatter_dimension=0, tiled=True
    ).astype(jnp.float32)
    qkv_grad, out_grad = weight_grads[:, : 3 * D], weight_grads[:, 3 * D : 4 * D]
    router_grad = weight_grads[:, 4 * D : 4 * D + experts_total]
    normed_grad = jnp.einsum(
        "qe,de->qd", projected_grad, qkv_full, preferred_element_type=jnp.float32
    )
    input_norm_grad, gain_one = norm_backward(normed_grad, normal_one, inverse_one, norm_gains[0])
    input_grad = (middle_grad + input_norm_grad).astype(jnp.bfloat16)[None]
    gains_grad, table_grad = lax.psum(
        (jnp.stack([gain_one, gain_two]), jnp.sum(bucket_rows, axis=-1).T), everywhere
    )
    return (
        layer_out,
        input_grad,
        qkv_grad,
        out_grad,
        router_grad,
        w_in_grad,
        w_out_grad,
        gains_grad,
        table_grad,
    )


def solution(mesh):
    return jax.shard_map(
        local,
        mesh=mesh,
        in_specs=(
            P(("dp", "expert"), "seq", None),
            P(("dp", "seq", "expert"), None),
            P(("dp", "seq", "expert"), None),
            P(("dp", "seq", "expert"), None),
            P("expert", ("dp", "seq"), None),
            P("expert", None, ("dp", "seq")),
            P(),
            P(),
            P(("dp", "expert"), "seq", None),
            P(("dp", "expert"), "seq", None),
        ),
        out_specs=(
            P(("dp", "expert"), "seq", None),
            P(("dp", "expert"), "seq", None),
            P(("dp", "seq", "expert"), None),
            P(("dp", "seq", "expert"), None),
            P(("dp", "seq", "expert"), None),
            P("expert", ("dp", "seq"), None),
            P("expert", None, ("dp", "seq")),
            P(),
            P(),
        ),
        check_vma=False,
    )
```

```python
import functools
import math

import jax
import jax.numpy as jnp
from jax import lax
from jax.experimental import pallas as pl
from jax.experimental.pallas import tpu as pltpu
from jax.sharding import PartitionSpec as P

D = 768
HEADS = 12
HEAD_DIM = 64
FF = 3072
BUCKETS = 32
LEN_DEV = 256


EPS = 1e-06
HIGH_PRECISION = lax.Precision.HIGHEST
CONTRACT_ROWS = (((0,), (0,)), ((), ()))


def bucket_edges(bucket_count):
    exact_count = bucket_count // 2
    boundaries = list(range(1, exact_count + 1))
    for bucket_index in range(exact_count + 1, bucket_count):
        power = (bucket_index - exact_count) / (bucket_count - exact_count)
        boundaries.append(math.ceil(exact_count * (128.0 / exact_count) ** power))
    return boundaries


def bucket_ids(distance, bucket_count):
    distance = jnp.maximum(distance, 0)
    bucket_sum = jnp.zeros(distance.shape, jnp.int32)
    for boundary in bucket_edges(bucket_count):
        bucket_sum = bucket_sum + (distance >= boundary).astype(jnp.int32)
    return bucket_sum


def norm_forward(values, scale_gain):
    inverse = lax.rsqrt(jnp.mean(values * values, axis=-1, keepdims=True) + EPS)
    normal_rows = values * inverse
    return (normal_rows * scale_gain, normal_rows, inverse)


def norm_backward(grad_out, normal_rows, inverse, scale_gain):
    gain_part = jnp.sum(grad_out * normal_rows, axis=0)
    scaled = grad_out * scale_gain
    value_grad = inverse * (
        scaled - normal_rows * jnp.mean(scaled * normal_rows, axis=-1, keepdims=True)
    )
    return (value_grad, gain_part)


def to_slots(slot_table, rows):
    return jnp.dot(slot_table, rows, preferred_element_type=jnp.float32).astype(jnp.bfloat16)


def from_slots(slot_table, rows):
    return lax.dot_general(slot_table, rows, CONTRACT_ROWS, preferred_element_type=jnp.float32)


TILE = 128
PAIR = 128
MASKED = -1e30
MATMUL_NT = (((1,), (1,)), ((), ()))


def matmul(left, right, dims=(((1,), (0,)), ((), ()))):
    return lax.dot_general(left, right, dims, preferred_element_type=jnp.float32)


def band_distance():
    key_row = lax.broadcasted_iota(jnp.int32, (2 * TILE, TILE), 0)
    query_column = lax.broadcasted_iota(jnp.int32, (2 * TILE, TILE), 1)
    return TILE + query_column - key_row


def fill_bias(strip, table_ref, head, tiles):
    distance = band_distance()
    band = jnp.full((2 * TILE, TILE), table_ref[0, head], jnp.float32)
    for bucket, edge in enumerate(bucket_edges(BUCKETS)):
        band = jnp.where(distance >= edge, table_ref[bucket + 1, head], band)
    band = jnp.where(distance >= 0, band, MASKED)
    far = (tiles - 2) * TILE
    strip[0:far, :] = jnp.full((far, TILE), table_ref[BUCKETS - 1, head], jnp.float32)
    strip[far : far + 2 * TILE, :] = band


def head_probabilities(strip, place, queries, keys, tiles):
    scores = matmul(keys, queries, MATMUL_NT)
    columns = []
    for part in range(LEN_DEV // TILE):
        blocks = []
        for slot in range(tiles * TILE // LEN_DEV):
            owner = jnp.bitwise_xor(place, slot)
            start = (tiles - 1 - part) * TILE + (owner - place) * LEN_DEV
            blocks.append(strip[pl.ds(pl.multiple_of(start, TILE), LEN_DEV), :])
        columns.append(jnp.concatenate(blocks, axis=0))
    scores = scores + jnp.concatenate(columns, axis=1)
    exps = jnp.exp(scores - jnp.max(scores, axis=0, keepdims=True))
    return exps * (1.0 / jnp.sum(exps, axis=0, keepdims=True))


def lane_halves(shape):
    return lax.broadcasted_iota(jnp.int32, shape, 1) < HEAD_DIM


def attend_kernel(tiles, place_ref, table_ref, q_ref, k_ref, v_ref, out_ref, strip):
    pair = pl.program_id(0)
    place = place_ref[0]

    @pl.when(pair == 0)
    def _():
        strip[tiles * TILE :, :] = jnp.full(((tiles - 1) * TILE, TILE), MASKED, jnp.float32)

    keys, values = k_ref[...], v_ref[...]
    queries = q_ref[...] * jnp.bfloat16(HEAD_DIM**-0.5)
    first = lane_halves(queries.shape)
    zero = jnp.zeros_like(queries)
    results = []
    for half in range(2):
        fill_bias(strip, table_ref, pair * 2 + half, tiles)
        own = jnp.where(first, queries, zero) if half == 0 else jnp.where(first, zero, queries)
        probs = head_probabilities(strip, place, own, keys, tiles).astype(jnp.bfloat16)
        results.append(matmul(values, probs, CONTRACT_ROWS))
    top = lax.broadcasted_iota(jnp.int32, results[0].shape, 0) < HEAD_DIM
    out_ref[...] = jnp.where(top, results[0], results[1]).T.astype(out_ref.dtype)


def attend_back_kernel(
    tiles, place_ref, table_ref, q_ref, k_ref, v_ref, g_ref, dq_ref, dkv_ref, sums_ref, strip, held
):
    pair = pl.program_id(0)
    place = place_ref[0]

    @pl.when(pair == 0)
    def _():
        strip[tiles * TILE :, :] = jnp.full(((tiles - 1) * TILE, TILE), MASKED, jnp.float32)

    keys, values = k_ref[...], v_ref[...]
    queries = q_ref[...] * jnp.bfloat16(HEAD_DIM**-0.5)
    grads = g_ref[...]
    first = lane_halves(queries.shape)
    zero = jnp.zeros_like(queries)
    distance = band_distance()
    buckets = jnp.full(distance.shape, -1, jnp.int32)
    for bucket, edge in enumerate([0] + bucket_edges(BUCKETS)):
        buckets = jnp.where(distance >= edge, bucket, buckets)
    q_parts, k_parts, v_parts = [], [], []
    for half in range(2):
        fill_bias(strip, table_ref, pair * 2 + half, tiles)
        own = jnp.where(first, queries, zero) if half == 0 else jnp.where(first, zero, queries)
        own_grads = jnp.where(first, grads, zero) if half == 0 else jnp.where(first, zero, grads)
        probs = head_probabilities(strip, place, own, keys, tiles)
        prob_grad = matmul(values, own_grads, MATMUL_NT)
        dots = jnp.sum(probs * prob_grad, axis=0, keepdims=True)
        score_grad = (probs * (prob_grad - dots)).astype(jnp.bfloat16)
        held[...] = score_grad
        k_parts.append(matmul(score_grad, queries))
        v_parts.append(matmul(probs.astype(jnp.bfloat16), grads))
        q_parts.append(matmul(keys, score_grad, CONTRACT_ROWS))
        band = jnp.zeros((2 * TILE, TILE), jnp.float32)
        for part in range(LEN_DEV // TILE):
            cols = slice(part * TILE, (part + 1) * TILE)
            same = score_grad[part * TILE : (part + 1) * TILE, cols].astype(jnp.float32)
            if part > 0:
                near = score_grad[(part - 1) * TILE : part * TILE, cols].astype(jnp.float32)
            else:
                slot = jnp.bitwise_xor(place, jnp.maximum(place - 1, 0))
                start = (slot + 1) * LEN_DEV - TILE
                near = held[pl.ds(pl.multiple_of(start, TILE), TILE), cols].astype(jnp.float32)
                near = jnp.where(place > 0, near, 0.0)
            band = band + jnp.concatenate([near, same], axis=0)
        total = jnp.sum(score_grad.astype(jnp.float32), axis=0, keepdims=True)
        total = total[:, :TILE] + total[:, TILE:]
        far = total - jnp.sum(band, axis=0, keepdims=True)
        for bucket in range(BUCKETS):
            row = jnp.sum(jnp.where(buckets == bucket, band, 0.0), axis=0, keepdims=True)
            if bucket == BUCKETS - 1:
                row = row + far
            sums_ref[half, bucket : bucket + 1, :] = row
    top = lax.broadcasted_iota(jnp.int32, q_parts[0].shape, 0) < HEAD_DIM
    dq = jnp.where(top, q_parts[0], q_parts[1]).T * HEAD_DIM**-0.5
    dq_ref[...] = dq.astype(dq_ref.dtype)
    side = lane_halves(k_parts[0].shape)
    for index, parts in enumerate((k_parts, v_parts)):
        both = jnp.where(side, parts[0], parts[1]).astype(dkv_ref.dtype)
        for slot in range(dkv_ref.shape[0]):
            dkv_ref[slot, index] = both[slot * LEN_DEV : (slot + 1) * LEN_DEV]


def attention_specs(full_length):
    pairs = D // PAIR
    smem = pl.BlockSpec(memory_space=pltpu.SMEM)
    rows = pl.BlockSpec((LEN_DEV, PAIR), lambda pair: (0, pair))
    keys = pl.BlockSpec((full_length, PAIR), lambda pair: (0, pair))
    values = pl.BlockSpec((full_length, PAIR), lambda pair: (0, pair + pairs))
    return pairs, smem, rows, keys, values


def attend(place, bias_table, projected, key_values):
    full_length = key_values.shape[0]
    tiles = full_length // TILE
    pairs, smem, rows, keys, values = attention_specs(full_length)
    return pl.pallas_call(
        functools.partial(attend_kernel, tiles),
        grid=(pairs,),
        out_shape=jax.ShapeDtypeStruct((LEN_DEV, D), jnp.bfloat16),
        in_specs=[smem, smem, rows, keys, values],
        out_specs=rows,
        scratch_shapes=[pltpu.VMEM(((2 * tiles - 1) * TILE, TILE), jnp.float32)],
        compiler_params=pltpu.CompilerParams(vmem_limit_bytes=40 * 2**20),
        cost_estimate=pl.CostEstimate(
            flops=4 * LEN_DEV * full_length * PAIR * HEADS,
            bytes_accessed=2 * D * (2 * LEN_DEV + 2 * full_length),
            transcendentals=HEADS * LEN_DEV * full_length,
        ),
    )(place, bias_table, projected, key_values, key_values)


def attend_back(place, bias_table, projected, key_values, attended_grad):
    full_length = key_values.shape[0]
    tiles = full_length // TILE
    pairs, smem, rows, keys, values = attention_specs(full_length)
    return pl.pallas_call(
        functools.partial(attend_back_kernel, tiles),
        grid=(pairs,),
        out_shape=(
            jax.ShapeDtypeStruct((LEN_DEV, D), jnp.bfloat16),
            jax.ShapeDtypeStruct((full_length // LEN_DEV, 2, LEN_DEV, D), jnp.bfloat16),
            jax.ShapeDtypeStruct((HEADS, BUCKETS, TILE), jnp.float32),
        ),
        in_specs=[smem, smem, rows, keys, values, rows],
        out_specs=(
            rows,
            pl.BlockSpec(
                (full_length // LEN_DEV, 2, LEN_DEV, PAIR), lambda pair: (0, 0, 0, pair)
            ),
            pl.BlockSpec((2, BUCKETS, TILE), lambda pair: (pair, 0, 0)),
        ),
        scratch_shapes=[
            pltpu.VMEM(((2 * tiles - 1) * TILE, TILE), jnp.float32),
            pltpu.VMEM((full_length, LEN_DEV), jnp.bfloat16),
        ],
        compiler_params=pltpu.CompilerParams(vmem_limit_bytes=48 * 2**20),
        cost_estimate=pl.CostEstimate(
            flops=10 * LEN_DEV * full_length * PAIR * HEADS,
            bytes_accessed=2 * D * (3 * LEN_DEV + 4 * full_length),
            transcendentals=HEADS * LEN_DEV * full_length,
        ),
    )(place, bias_table, projected, key_values, key_values, attended_grad)


def swap_pairs(block, bit):
    pairs = [(index, index ^ bit) for index in range(lax.axis_size("seq"))]
    return lax.ppermute(block, "seq", pairs)


def spread_sequence(block):
    held = {0: block}
    bit = lax.axis_size("seq") // 2
    while bit:
        held.update({slot ^ bit: swap_pairs(held[slot], bit) for slot in list(held)})
        bit //= 2
    return [held[slot] for slot in range(len(held))]


def sum_sequence(parts):
    held = {slot: parts[slot] for slot in range(parts.shape[0])}
    bit = 1
    while bit < parts.shape[0]:
        kept = {}
        for slot in held:
            if not slot & bit:
                arrived = swap_pairs(held[slot ^ bit].astype(jnp.bfloat16), bit)
                kept[slot] = held[slot].astype(jnp.float32) + arrived.astype(jnp.float32)
        held = kept
        bit *= 2
    return held[0].astype(jnp.bfloat16)


def swap_experts(slots, experts_total):
    return lax.all_to_all(
        slots.reshape(experts_total, slots.shape[0] // experts_total, slots.shape[1]),
        "expert",
        split_axis=0,
        concat_axis=0,
        tiled=True,
    ).reshape(slots.shape)


def local(
    tokens,
    qkv_weight,
    out_weight,
    router_weight,
    w_in,
    w_out,
    norm_gains,
    bias_table,
    expert_ids,
    cotangent,
):
    everywhere = ("dp", "seq", "expert")
    inputs = tokens[0].astype(jnp.float32)
    experts_total = lax.axis_size("expert")
    capacity = 3 * LEN_DEV // experts_total
    router_pad = jnp.zeros((router_weight.shape[0], PAIR - experts_total), jnp.bfloat16)
    packed = jnp.concatenate([qkv_weight, out_weight, router_weight, router_pad], axis=1)
    packed = lax.all_gather(packed, "expert", axis=0, tiled=True)
    packed = lax.all_gather(packed, ("dp", "seq"), axis=0, tiled=True)
    qkv_full, out_full = packed[:, : 3 * D], packed[:, 3 * D : 4 * D]
    router_full = packed[:, 4 * D : 4 * D + experts_total]

    route_ids = expert_ids[0]
    expert_names = jnp.arange(experts_total, dtype=jnp.int32)
    choose = (route_ids[..., None] == expert_names).astype(jnp.float32)
    flat_ids = route_ids.reshape(-1)
    expert_hits = (flat_ids[:, None] == expert_names).astype(jnp.int32)
    slot_rank = jnp.sum((jnp.cumsum(expert_hits, axis=0) - 1) * expert_hits, axis=-1)
    places = (flat_ids * capacity + slot_rank).reshape(LEN_DEV, 2)
    slot_index = jnp.arange(experts_total * capacity, dtype=jnp.int32)[:, None]
    hits = [slot_index == places[None, :, k] for k in range(2)]
    tables = [hit.astype(jnp.bfloat16) for hit in hits]
    token_table = (hits[0] | hits[1]).astype(jnp.bfloat16)
    arrived_cotangent = swap_experts(to_slots(token_table, cotangent[0]), experts_total)

    normalized_rows, normal_one, inverse_one = norm_forward(inputs, norm_gains[0])
    normed_low = normalized_rows.astype(jnp.bfloat16)
    normed_low, arrived_cotangent = lax.optimization_barrier((normed_low, arrived_cotangent))
    projected_rows = jnp.dot(normed_low, qkv_full, preferred_element_type=jnp.float32).astype(
        jnp.bfloat16
    )
    key_values = jnp.concatenate(spread_sequence(projected_rows[:, D:]), axis=0)
    place = lax.axis_index("seq").astype(jnp.int32).reshape(1)
    attended_low = attend(place, bias_table, projected_rows, key_values)
    w_in_full = lax.all_gather(w_in, ("dp", "seq"), axis=1, tiled=True)[0]
    w_out_full = lax.all_gather(w_out, ("dp", "seq"), axis=2, tiled=True)[0]
    middle = inputs + jnp.dot(attended_low, out_full, preferred_element_type=jnp.float32)
    mixed, normal_two, inverse_two = norm_forward(middle, norm_gains[1])
    mixed_low = mixed.astype(jnp.bfloat16)
    expert_rows = swap_experts(to_slots(token_table, mixed_low), experts_total)
    router_logits = jnp.dot(mixed_low, router_full, preferred_element_type=jnp.float32)
    chosen = jnp.sum(choose * router_logits[:, None, :], axis=-1)
    gate_weights = jax.nn.softmax(chosen, axis=-1)
    gate_slots = jnp.sum(
        jnp.where(hits[0], gate_weights[None, :, 0], 0.0)
        + jnp.where(hits[1], gate_weights[None, :, 1], 0.0),
        axis=1,
    )
    gate_slots, expert_rows = lax.optimization_barrier((gate_slots, expert_rows))
    arrived_gates = lax.all_to_all(
        gate_slots.reshape(experts_total, capacity),
        "expert",
        split_axis=0,
        concat_axis=0,
        tiled=True,
    ).reshape(-1, 1)
    pre_act = jnp.dot(expert_rows, w_in_full, preferred_element_type=jnp.float32)
    hidden_low = jax.nn.gelu(pre_act).astype(jnp.bfloat16)
    expert_out = jnp.dot(hidden_low, w_out_full, preferred_element_type=jnp.float32).astype(
        jnp.bfloat16
    )
    returned = swap_experts(expert_out, experts_total)
    arrived_grad = (arrived_gates * arrived_cotangent.astype(jnp.float32)).astype(jnp.bfloat16)
    hidden_grad = jnp.einsum(
        "rd,fd->rf", arrived_grad, w_out_full, preferred_element_type=jnp.float32
    )
    gelu_value, gelu_pull = jax.vjp(jax.nn.gelu, pre_act)
    pre_grad = gelu_pull(hidden_grad)[0].astype(jnp.bfloat16)
    row_grad = jnp.einsum(
        "rf,df->rd", pre_grad, w_in_full, preferred_element_type=jnp.float32
    ).astype(jnp.bfloat16)
    row_grad, pre_grad, hidden_low = lax.optimization_barrier((row_grad, pre_grad, hidden_low))
    returned_grad = swap_experts(row_grad, experts_total)
    first_term = lax.dot_general(
        expert_rows, pre_grad, CONTRACT_ROWS, preferred_element_type=jnp.float32
    ).astype(jnp.bfloat16)
    second_term = lax.dot_general(
        arrived_grad, hidden_low, CONTRACT_ROWS, preferred_element_type=jnp.float32
    ).astype(jnp.bfloat16)

    expert_terms = jnp.concatenate([first_term, second_term], axis=1)
    returned, expert_terms = lax.optimization_barrier((returned, expert_terms))
    upstream = cotangent[0].astype(jnp.float32)
    gathered = [from_slots(table, returned) for table in tables]
    block_out = middle + gate_weights[:, :1] * gathered[0] + gate_weights[:, 1:] * gathered[1]
    layer_out = block_out.astype(jnp.bfloat16)[None]
    gate_grad = jnp.stack([jnp.sum(upstream * rows, axis=-1) for rows in gathered], axis=-1)
    gate_mean = jnp.sum(gate_weights * gate_grad, axis=-1, keepdims=True)
    chosen_grad = gate_weights * (gate_grad - gate_mean)
    logit_grad = jnp.sum(choose * chosen_grad[..., None], axis=1)
    router_part = lax.dot_general(
        mixed_low.astype(jnp.float32), logit_grad, CONTRACT_ROWS, precision=HIGH_PRECISION
    )
    copy_back = from_slots(token_table, returned_grad)
    mixed_grad = copy_back + jnp.dot(
        logit_grad, router_full.astype(jnp.float32).T, precision=HIGH_PRECISION
    )
    middle_norm_grad, gain_two = norm_backward(mixed_grad, normal_two, inverse_two, norm_gains[1])
    middle_grad = upstream + middle_norm_grad
    branch_low = middle_grad.astype(jnp.bfloat16)
    attended_grad = jnp.einsum(
        "qe,de->qd", branch_low, out_full, preferred_element_type=jnp.float32
    ).astype(jnp.bfloat16)
    query_grad, kv_part, bucket_rows = attend_back(
        place, bias_table, projected_rows, key_values, attended_grad
    )
    kv_grad = sum_sequence(kv_part)
    out_part = lax.dot_general(
        attended_low, branch_low, CONTRACT_ROWS, preferred_element_type=jnp.float32
    )
    expert_grad = lax.psum_scatter(
        expert_terms, ("dp", "seq"), scatter_dimension=0, tiled=True
    )
    projected_grad = jnp.concatenate([query_grad, kv_grad[0], kv_grad[1]], axis=1)
    projected_grad, expert_grad = lax.optimization_barrier((projected_grad, expert_grad))
    w_in_grad = expert_grad[:, :FF].astype(jnp.float32)[None]
    w_out_grad = expert_grad[:, FF:].astype(jnp.float32).T[None]
    qkv_part = lax.dot_general(
        normed_low, projected_grad, CONTRACT_ROWS, preferred_element_type=jnp.float32
    )
    router_part = jnp.pad(router_part, ((0, 0), (0, PAIR - experts_total)))
    weight_parts = jnp.concatenate([qkv_part, out_part, router_part], axis=1)
    weight_grads = lax.psum_scatter(
        weight_parts.astype(jnp.bfloat16), ("dp", "seq"), scatter_dimension=0, tiled=True
    )
    weight_grads = swap_experts(weight_grads, experts_total)
    weight_grads = jnp.sum(
        weight_grads.reshape(experts_total, -1, weight_grads.shape[1]).astype(jnp.float32), axis=0
    )
    qkv_grad, out_grad = weight_grads[:, : 3 * D], weight_grads[:, 3 * D : 4 * D]
    router_grad = weight_grads[:, 4 * D : 4 * D + experts_total]
    normed_grad = jnp.einsum(
        "qe,de->qd", projected_grad, qkv_full, preferred_element_type=jnp.float32
    )
    input_norm_grad, gain_one = norm_backward(normed_grad, normal_one, inverse_one, norm_gains[0])
    input_grad = (middle_grad + input_norm_grad).astype(jnp.bfloat16)[None]
    gains_grad, table_grad = lax.psum(
        (jnp.stack([gain_one, gain_two]), jnp.sum(bucket_rows, axis=-1).T), everywhere
    )
    return (
        layer_out,
        input_grad,
        qkv_grad,
        out_grad,
        router_grad,
        w_in_grad,
        w_out_grad,
        gains_grad,
        table_grad,
    )


def solution(mesh):
    return jax.shard_map(
        local,
        mesh=mesh,
        in_specs=(
            P(("dp", "expert"), "seq", None),
            P(("dp", "seq", "expert"), None),
            P(("dp", "seq", "expert"), None),
            P(("dp", "seq", "expert"), None),
            P("expert", ("dp", "seq"), None),
            P("expert", None, ("dp", "seq")),
            P(),
            P(),
            P(("dp", "expert"), "seq", None),
            P(("dp", "expert"), "seq", None),
        ),
        out_specs=(
            P(("dp", "expert"), "seq", None),
            P(("dp", "expert"), "seq", None),
            P(("dp", "seq", "expert"), None),
            P(("dp", "seq", "expert"), None),
            P(("dp", "seq", "expert"), None),
            P("expert", ("dp", "seq"), None),
            P("expert", None, ("dp", "seq")),
            P(),
            P(),
        ),
        check_vma=False,
    )
```
